32 devices in a mesh: node: 4 (over y, x), local: 8 (over z, core).
Axes of the slice: x: 2, y: 2, z: 4, core: 2. Of those that a mesh axis runs over, the one named last changes fastest.
Arguments:
- tokens: bfloat16 [4096, 7168], P(('node', 'local')), may hold values from -6 to 6
- route_ids: int32 [4096, 8], P(('node', 'local')), may hold values from 0 to 383, all different within a row; in each aligned block of 128 rows (0 to 127, 128 to 255, ...) at most 5 rows name the same one
- route_gates: bfloat16 [4096, 8], P(('node', 'local')), may hold values from 0.099609375 to 1
- limits: int32 [384], replicated, may hold values from 1 to 5, as said below
- w_gate: bfloat16 [32, 7168, 448], P(('node', 'local')), may hold values from -0.0625 to 0.0625
- w_up: bfloat16 [32, 7168, 448], P(('node', 'local')), may hold values from -0.0625 to 0.0625
- w_down: bfloat16 [32, 448, 7168], P(('node', 'local')), may hold values from -0.125 to 0.125
Outputs:
- mixed: bfloat16 [4096, 7168], P(('node', 'local'))
The draws below stay inside these ranges and needn't reach their ends.
Inputs may be any that keep to these rules, and one draw needn't show every extreme that they name: `route_ids`: in each aligned block of 128 rows (the rows of one device) no expert is named by more than 5 rows, a bound that some block reaches; a row names 8 different experts. `limits`: some expert's capacity is exactly 5.
All inputs are finite; a program needn't handle non-finite values.
Results may differ from the reference program's by a relative error of at most 0.0057.
Values may be sent and summed in bfloat16 or wider, within the bound.
A program may use at most 128 MiB of HBM per device.

```python
import math
import jax
import jax.numpy as jnp
import numpy as np
from jax import lax

D = 7168
EXPERTS = 384
TOP = 8
FF_WIN = 1792
TOK_DEV = 128
GROUP = 4
CAP = 5
FF_SLAB = 448
EXP_HOST = 8
SLABS = 32
TOKENS = 4096


def draw_limits(key, part):
    key = jax.random.fold_in(key, 7)
    base_key, spot_key = jax.random.split(key)
    drawn = jax.random.randint(base_key, (EXPERTS,), 1, CAP + 1, dtype=jnp.int32)
    position = jax.random.randint(spot_key, (), 0, EXP_HOST, dtype=jnp.int32)
    return drawn.at[position].set(CAP)


def block_levels(rng, extent, cuts, least, largest):
    def one(dim, blocks):
        steps = jax.random.uniform(jax.random.fold_in(jax.random.fold_in(rng, 6), dim), (blocks,), jnp.float32, least / len(cuts), largest / len(cuts))
        return jnp.repeat(jnp.exp(steps), extent[dim] // blocks).reshape((-1,) + (1,) * (len(extent) - dim - 1))

    level = one(*cuts[0])
    for cut in cuts[1:]:
        level = level * one(*cut)
    return level


def shared_out(own_key, own, number, rows, count, top, bound, lean):
    ranking = jax.random.permutation(own_key, count)
    packed, usual = shares(count, rows * top, bound, lean, True), shares(count, rows * top, bound, lean, False)
    places = jnp.arange(count)

    def named(sizes, turn):
        used = int((sizes > 0).sum())
        fixed = max(1, used // 4)
        moved = fixed + (places - fixed + turn * (used - fixed)) % max(1, count - fixed)
        return jnp.zeros((count,), jnp.int32).at[ranking[jnp.where(places < fixed, places, moved)]].set(jnp.asarray(sizes, jnp.int32))

    sizes = jnp.where(number % 4 == 0, named(packed, number // 4), named(usual, number - number // 4 - 1))
    mixed = jax.random.permutation(jax.random.fold_in(own, 3), count)
    source_of, receiver = mixed[0:count // 2 * 2:2], mixed[1:count // 2 * 2:2]
    slack = jnp.minimum(sizes[source_of] - 1, bound - sizes[receiver]) // 2
    slack = jnp.where((source_of == ranking[0]) | (receiver == ranking[0]) | (sizes[receiver] == 0), 0, jnp.maximum(slack, 0))
    moved = jax.random.randint(jax.random.fold_in(own, 4), (count // 2,), 0, 1 << 20) % (slack + 1)
    sizes = sizes.at[source_of].add(-moved).at[receiver].add(moved)
    labels = jnp.searchsorted(jnp.cumsum(sizes), jnp.arange(rows * top), side="right").astype(jnp.int32)
    table = labels.reshape(top, rows).T
    table = table[jax.random.permutation(jax.random.fold_in(own, 1), rows)]
    turn = jax.random.randint(jax.random.fold_in(own, 2), (rows, 1), 0, top)
    return jnp.take_along_axis(table, (jnp.arange(top)[None, :] + turn) % top, axis=1)


def shares(number_of, total, limit, skew, full):
    weights = [(1 << 20) // math.isqrt(rank ** skew) + 1 for rank in range(1, number_of + 1)]
    largest = limit if full else min(limit, max(-(-total // number_of), total * weights[0] // sum(weights)))
    least = 1 if total - largest >= number_of - 1 else 0
    given, spare = [largest] + [least] * (number_of - 1), total - largest - least * (number_of - 1)
    while spare > 0:
        candidates = [i for i in range(1, number_of) if given[i] < largest] or [i for i in range(1, number_of) if given[i] < limit]
        mass, remaining = sum([weights[i] for i in candidates]), spare
        for i in candidates:
            addition = min(limit - given[i], max(1, remaining * weights[i] // mass), spare)
            given[i] = given[i] + addition
            spare = spare - addition
    return np.array(given)


def gaussian(stream_key, shape, deviation, limit, cuts=(), kind=jnp.bfloat16):
    result = jax.random.normal(stream_key, shape, jnp.float32) * deviation
    if len(cuts) > 0:
        result = block_levels(stream_key, shape, cuts, -0.22, 0.18) * result
    return jnp.clip(result, min=-limit, max=limit).astype(kind)


def setup_inputs(seed: int = 0) -> dict:
    arg_keys = jax.random.split(jax.random.key(seed), 8)
    tokens = gaussian(arg_keys[0], (TOKENS, D), 1.0, 6.0, ((0, 32),))
    route_ids_keys = jax.random.split(jax.random.fold_in(arg_keys[1], 1), TOKENS // TOK_DEV)
    route_ids_turns = jax.random.permutation(jax.random.fold_in(arg_keys[1], 3), TOKENS // TOK_DEV)
    route_ids = jax.vmap(lambda own, number: shared_out(jax.random.fold_in(arg_keys[1], 2), own, number, TOK_DEV, EXPERTS, TOP, CAP, 2))(route_ids_keys, route_ids_turns).reshape((TOKENS, TOP))
    route_gates = jnp.clip(jnp.exp(math.log(1.0) - 2.306499 * jax.random.uniform(arg_keys[2], (TOKENS, TOP), jnp.float32) ** block_levels(arg_keys[2], (TOKENS, TOP), ((0, 32),), -0.2, 0.2)), 0.099609375, 1.0).astype(jnp.bfloat16)
    limits = draw_limits(jax.random.fold_in(arg_keys[7], 71), 0)
    w_gate = gaussian(arg_keys[4], (SLABS, D, FF_SLAB), D ** -0.5, 0.0625, ((0, 32),))
    w_up = gaussian(arg_keys[5], (SLABS, D, FF_SLAB), D ** -0.5, 0.0625, ((0, 32),))
    w_down = gaussian(arg_keys[6], (SLABS, FF_SLAB, D), FF_WIN ** -0.5, 0.125, ((0, 32),))
    return dict(tokens=tokens, route_ids=route_ids, route_gates=route_gates, limits=limits, w_gate=w_gate, w_up=w_up, w_down=w_down)


def reference(tokens, route_ids, route_gates, limits, w_gate, w_up, w_down):
    blocks = TOKENS // TOK_DEV
    experts = jnp.arange(EXP_HOST, dtype=jnp.int32)
    matches = route_ids[:, :, None] == experts[None, None, :]
    per_tok = jnp.sum(matches.astype(jnp.int32), axis=1).astype(jnp.int32)
    per_block = per_tok.reshape(blocks, TOK_DEV, EXP_HOST)
    before = (jnp.cumsum(per_block, axis=1).astype(jnp.int32) - per_block).reshape(TOKENS, EXP_HOST)
    keep_mask = (per_tok > 0) & (before < limits[None, :EXP_HOST])
    gate_sum = jnp.sum(jnp.where(matches, route_gates.astype(jnp.float32)[:, :, None], jnp.float32(0.0)), axis=1)
    coef = jnp.where(keep_mask, gate_sum, jnp.float32(0.0))
    block_of = (jnp.arange(TOKENS, dtype=jnp.int32) // TOK_DEV).astype(jnp.int32)
    slot_of = jnp.where(keep_mask, block_of[:, None] * CAP + before, blocks * CAP).astype(jnp.int32)
    token_ids = jnp.broadcast_to(jnp.arange(TOKENS, dtype=jnp.int32)[:, None], (TOKENS, EXP_HOST))
    expert_ids = jnp.broadcast_to(experts[None, :], (TOKENS, EXP_HOST))
    row_index = jnp.zeros((EXP_HOST, blocks * CAP), jnp.int32).at[expert_ids, slot_of].set(token_ids, mode="drop")
    row_coef = jnp.zeros((EXP_HOST, blocks * CAP), jnp.float32).at[expert_ids, slot_of].set(coef, mode="drop")
    gate_all = w_gate.reshape(EXP_HOST, GROUP, D, FF_SLAB)
    up_all = w_up.reshape(EXP_HOST, GROUP, D, FF_SLAB)
    down_all = w_down.reshape(EXP_HOST, GROUP, FF_SLAB, D)

    def add_expert(total, pieces):
        gate_w, up_w, down_w, indices, coef_rows = pieces
        gathered = tokens[indices].astype(jnp.float32)
        gate_act = jnp.einsum("rd,sdf->srf", gathered, gate_w.astype(jnp.float32), precision=lax.Precision.HIGHEST)
        upper = jnp.einsum("rd,sdf->srf", gathered, up_w.astype(jnp.float32), precision=lax.Precision.HIGHEST)
        hidden = lax.optimization_barrier((jax.nn.silu(gate_act) * upper).astype(jnp.bfloat16))
        parts = jnp.einsum("srf,sfd->srd", hidden.astype(jnp.float32), down_w.astype(jnp.float32), precision=lax.Precision.HIGHEST)
        parts = lax.optimization_barrier(parts.astype(jnp.bfloat16))
        expert_out = jnp.sum(parts.astype(jnp.float32), axis=0)
        total = total.at[indices].add(coef_rows[:, None] * expert_out)
        return total, None

    total, _ = lax.scan(add_expert, jnp.zeros((TOKENS, D), jnp.float32), (gate_all, up_all, down_all, row_index, row_coef))
    return total.astype(jnp.bfloat16)
```

```python
import functools

import jax
import jax.numpy as jnp
from jax import lax
from jax.experimental import pallas as pl
from jax.experimental.pallas import tpu as pltpu
from jax.sharding import PartitionSpec as P

GROUP = 4
CAP = 5
SUB = 16
SPLIT = 3
COL = 256
BF = jnp.bfloat16
F32 = jnp.float32
MESH = pl.DeviceIdType.MESH


def dot(a, b):
    return jnp.dot(a, b, preferred_element_type=F32)


def dot_t(a, b):
    return lax.dot_general(a, b, (((1,), (1,)), ((), ())), preferred_element_type=F32)


def iota(shape, dim):
    return lax.broadcasted_iota(jnp.int32, shape, dim)


def div_cap(x):
    return (x * 205) >> 10


def kernel(
    dims,
    tok_hbm, ids_ref, gates_ref, limits_ref, wg_hbm, wu_hbm, wd_hbm,
    out_ref,
    tok, wg, wu, wd, pack, x, xu, own, sib, sib_in, par_in, home,
    in_sem, recv_x, send_d, send_s, send_r, send_p, recv_p, send_q, recv_q, send_h, recv_h,
):
    nodes, locs = dims
    groups = locs // GROUP
    units = locs // 2
    hosted = nodes * groups
    rows = tok.shape[0]
    width = tok.shape[1]
    piece = x.shape[-1]
    tail0 = SPLIT * piece
    cols = piece // COL
    packed = hosted * SUB
    srcs = 2 * nodes
    chunk = srcs * SUB
    xrows = xu.shape[0]

    node = lax.axis_index("node")
    loc = lax.axis_index("local")
    core = lax.rem(loc, 2)
    unit = loc // 2
    place = lax.rem(unit, 2)
    group = unit // 2
    sibling = (node, unit * 2 + (1 - core))
    partner = (node, group * GROUP + 2 * (1 - place) + core)

    loads = [
        pltpu.make_async_copy(tok_hbm, tok, in_sem.at[0]),
        pltpu.make_async_copy(wg_hbm, wg, in_sem.at[1]),
        pltpu.make_async_copy(wu_hbm, wu, in_sem.at[2]),
        pltpu.make_async_copy(wd_hbm, wd, in_sem.at[3]),
    ]
    for load in loads:
        load.start()

    barrier = pltpu.get_barrier_semaphore()

    def greet(i, _):
        n, u = i // units, lax.rem(i, units)

        @pl.when(jnp.logical_or(n != node, u != unit))
        def _():
            pl.semaphore_signal(barrier, inc=1, device_id=(n, u * 2 + core), device_id_type=MESH)

        return 0

    lax.fori_loop(0, nodes * units, greet, 0)
    pl.semaphore_signal(barrier, inc=1, device_id=sibling, device_id_type=MESH)

    ep = 128
    expert = iota((ep, rows), 0)
    named = jnp.zeros((ep, rows), F32)
    gate = jnp.zeros((ep, rows), F32)
    for k in range(ids_ref.shape[0]):
        hit = ids_ref[k : k + 1, :] == expert
        named = named + jnp.where(hit, 1.0, 0.0)
        gate = gate + jnp.where(hit, gates_ref[k : k + 1, :].astype(F32), 0.0)
    earlier = jnp.where(iota((rows, rows), 0) < iota((rows, rows), 1), 1.0, 0.0).astype(BF)
    before = dot(named.astype(BF), earlier)
    lim = jnp.where(iota((ep, ep), 0) == iota((ep, ep), 1), limits_ref[:, :ep].astype(F32), 0.0)
    lim = jnp.sum(lim, axis=1, keepdims=True)
    kept = jnp.logical_and(named > 0.5, before < lim)
    slot = jnp.where(kept, before, -1.0)
    coef = jnp.where(kept, gate, 0.0)
    spread = jnp.where(iota((packed, ep), 0) // SUB == iota((packed, ep), 1), 1.0, 0.0).astype(BF)
    slot_m = dot(spread, slot.astype(BF))
    coef_m = dot(spread, coef.astype(BF))

    def member(line, slots, q):
        row = lax.rem(line, SUB)
        rank = (row * 11) >> 5
        ok = jnp.logical_and(row < SUB - 1, row - SPLIT * rank == q)
        return jnp.logical_and(ok, slots == rank.astype(F32))

    def member_tail(line, slots, r):
        return jnp.logical_and(lax.rem(line, SUB) == SUB - 1, slots == float(r))

    line = iota((packed, rows), 0)
    heads = [jnp.where(member(line, slot_m, q), 1.0, 0.0).astype(BF) for q in range(SPLIT)]
    tails = [jnp.where(member_tail(line, slot_m, r), 1.0, 0.0).astype(BF) for r in range(CAP)]

    loads[0].wait()
    for j in range(cols):
        acc = dot(heads[0], tok[:, j * COL : (j + 1) * COL])
        for q in range(1, SPLIT):
            acc = acc + dot(heads[q], tok[:, q * piece + j * COL : q * piece + (j + 1) * COL])
        if j < CAP:
            acc = acc + dot(tails[j], tok[:, tail0:])
        pack[:, :, j * COL : (j + 1) * COL] = acc.astype(BF).reshape(hosted, SUB, COL)

    pl.semaphore_wait(barrier, nodes * units)

    def near_place(src_group, src_place, g):
        return jnp.where(src_group < g, 0, jnp.where(src_group > g, 1, src_place))

    def target(i):
        g = lax.rem(group + 1 + i // nodes, groups)
        n = lax.rem(node + 1 + lax.rem(i, nodes), nodes)
        to_unit = 2 * g + near_place(group, place, g)
        e = n * groups + g
        return e, n, to_unit, jnp.logical_and(n == node, to_unit == unit)

    def dispatch(e, n, to_unit):
        return pltpu.make_async_remote_copy(
            src_ref=pack.at[e], dst_ref=x.at[unit, core, node], send_sem=send_d.at[e],
            recv_sem=recv_x.at[unit, core, node], device_id=(n, 2 * to_unit + core), device_id_type=MESH,
        )

    def send_out(i, _):
        e, n, to_unit, mine = target(i)

        @pl.when(mine)
        def _():
            pltpu.make_async_copy(pack.at[e], x.at[unit, core, node], recv_x.at[unit, core, node]).start()

        @pl.when(jnp.logical_not(mine))
        def _():
            dispatch(e, n, to_unit).start()

        return 0

    lax.fori_loop(0, hosted, send_out, 0)

    at_row, at_line = iota((xrows, chunk), 0), iota((xrows, chunk), 1)
    first = SUB * div_cap(at_row)
    rank = at_row - CAP * div_cap(at_row)
    open_all = jnp.concatenate(
        [jnp.where(at_line == first + SPLIT * rank + q, 1.0, 0.0).astype(BF) for q in range(SPLIT)], axis=0
    )
    open_tail = [
        jnp.where(jnp.logical_and(at_line == first + SUB - 1, rank == r), 1.0, 0.0).astype(BF) for r in range(CAP)
    ]
    at_line, at_row = iota((chunk, xrows), 0), iota((chunk, xrows), 1)
    src = lax.rem(at_line // SUB + core * nodes, srcs)
    sub_row = lax.rem(at_line, SUB)
    rank_of = at_row - CAP * div_cap(at_row)
    same = src == div_cap(at_row)
    close = [
        jnp.where(jnp.logical_and(same, sub_row == SPLIT * rank_of + q), 1.0, 0.0).astype(BF) for q in range(SPLIT)
    ]
    close_tail = [
        jnp.where(jnp.logical_and(same, jnp.logical_and(sub_row == SUB - 1, rank_of == r)), 1.0, 0.0).astype(BF)
        for r in range(CAP)
    ]

    def unit_at(j):
        return lax.rem(2 * group + j, units)

    def is_near(u):
        return near_place(u // 2, lax.rem(u, 2), group) == place

    def to_sibling(u, n):
        return pltpu.make_async_remote_copy(
            src_ref=x.at[u, core, n], dst_ref=x.at[u, core, n], send_sem=send_s.at[u, n],
            recv_sem=recv_x.at[u, core, n], device_id=sibling, device_id_type=MESH,
        )

    def to_partner(u, n):
        return pltpu.make_async_remote_copy(
            src_ref=x.at[u, core, n], dst_ref=x.at[u, core, n], send_sem=send_r.at[u, n],
            recv_sem=recv_x.at[u, core, n], device_id=partner, device_id_type=MESH,
        )

    def give_half(j, u):
        return pltpu.make_async_remote_copy(
            src_ref=sib.at[lax.rem(j, 2)], dst_ref=sib_in.at[u], send_sem=send_p.at[lax.rem(j, 2)],
            recv_sem=recv_p.at[u], device_id=sibling, device_id_type=MESH,
        )

    def give_sum(u):
        return pltpu.make_async_remote_copy(
            src_ref=own.at[u], dst_ref=par_in.at[u], send_sem=send_q.at[u],
            recv_sem=recv_q.at[u], device_id=partner, device_id_type=MESH,
        )

    expert_here = node * groups + group

    def give_home(u, n):
        return pltpu.make_async_remote_copy(
            src_ref=own.at[u, n], dst_ref=home.at[expert_here], send_sem=send_h.at[u, n],
            recv_sem=recv_h.at[expert_here], device_id=(n, 2 * u + core), device_id_type=MESH,
        )

    def landed(ref, sem):
        pltpu.make_async_copy(ref, ref, sem).wait()

    def compute(j, u):
        tail = jnp.zeros((xrows, COL), F32)
        for c in range(cols):
            xc = x[u, :, :, :, c * COL : (c + 1) * COL].reshape(chunk, COL)
            opened = dot(open_all, xc).astype(BF)
            for q in range(SPLIT):
                xu[:, q * piece + c * COL : q * piece + (c + 1) * COL] = opened[q * xrows : (q + 1) * xrows]
            if c < CAP:
                tail = tail + dot(open_tail[c], xc)
        xu[:, tail0:] = tail.astype(BF)

        @pl.when(j == 0)
        def _():
            for load in loads[1:]:
                load.wait()

        act = dot_t(xu[...], wg[...])
        up = dot_t(xu[...], wu[...])
        hidden = (act / (1.0 + jnp.exp(-act)) * up).astype(BF)
        spreads = [dot(m, hidden).astype(BF) for m in close]
        last = dot(hidden, wd[:, tail0:]).astype(BF)
        b = lax.rem(j, 2)
        for c in range(cols):
            acc = dot(spreads[0], wd[:, c * COL : (c + 1) * COL])
            for q in range(1, SPLIT):
                acc = acc + dot(spreads[q], wd[:, q * piece + c * COL : q * piece + (c + 1) * COL])
            if c < CAP:
                acc = acc + dot(close_tail[c], last)
            parts = acc.astype(BF).reshape(2, nodes, SUB, COL)
            own[u, :, :, c * COL : (c + 1) * COL] = parts[0]
            sib[b, :, :, c * COL : (c + 1) * COL] = parts[1]

    def step(j, _):
        u = unit_at(j)

        @pl.when(j < units)
        def _():
            near = is_near(u)

            def relay(n, _):
                landed(x.at[u, core, n], recv_x.at[u, core, n])

                @pl.when(near)
                def _():
                    to_partner(u, n).start()

                to_sibling(u, n).start()
                return 0

            lax.fori_loop(0, nodes, relay, 0)

            def arrive(n, _):
                landed(x.at[u, 1 - core, n], recv_x.at[u, 1 - core, n])
                return 0

            lax.fori_loop(0, nodes, arrive, 0)

            @pl.when(j >= 2)
            def _():
                give_half(j, u).wait_send()

            compute(j, u)
            give_half(j, u).start()

        @pl.when(jnp.logical_and(j >= 1, j < units + 1))
        def _():
            v = unit_at(j - 1)
            landed(sib_in.at[v], recv_p.at[v])

            @pl.when(jnp.logical_not(is_near(v)))
            def _():
                for n in range(nodes):
                    own[v, n] = (own[v, n].astype(F32) + sib_in[v, n].astype(F32)).astype(BF)
                give_sum(v).start()

        @pl.when(j >= 2)
        def _():
            v = unit_at(j - 2)

            @pl.when(is_near(v))
            def _():
                landed(par_in.at[v], recv_q.at[v])
                for n in range(nodes):
                    total = own[v, n].astype(F32) + sib_in[v, n].astype(F32) + par_in[v, n].astype(F32)
                    own[v, n] = total.astype(BF)

                def back(n, _):
                    mine = jnp.logical_and(n == node, v == unit)

                    @pl.when(mine)
                    def _():
                        pltpu.make_async_copy(own.at[v, n], home.at[expert_here], recv_h.at[expert_here]).start()

                    @pl.when(jnp.logical_not(mine))
                    def _():
                        give_home(v, n).start()

                    return 0

                lax.fori_loop(0, nodes, back, 0)

        return 0

    lax.fori_loop(0, units + 2, step, 0)

    line = iota((rows, packed), 1)
    slot_t = jnp.transpose(slot_m)
    coef_t = jnp.transpose(coef_m)
    heads = [jnp.where(member(line, slot_t, q), coef_t, 0.0).astype(BF) for q in range(SPLIT)]
    tails = [jnp.where(member_tail(line, slot_t, r), coef_t, 0.0).astype(BF) for r in range(CAP)]

    def returned(e, _):
        landed(home.at[e], recv_h.at[e])
        return 0

    lax.fori_loop(0, hosted, returned, 0)
    tail = jnp.zeros((rows, COL), F32)
    for c in range(cols):
        got = home[:, :, c * COL : (c + 1) * COL].reshape(packed, COL)
        for q in range(SPLIT):
            out_ref[:, q * piece + c * COL : q * piece + (c + 1) * COL] = dot(heads[q], got).astype(BF)
        if c < CAP:
            tail = tail + dot(tails[c], got)
    out_ref[:, tail0:] = tail.astype(BF)

    def sent(i, _):
        e, n, to_unit, mine = target(i)

        @pl.when(jnp.logical_not(mine))
        def _():
            dispatch(e, n, to_unit).wait_send()

        return 0

    lax.fori_loop(0, hosted, sent, 0)

    def drained(u, _):
        near = is_near(u)

        def each(n, _):
            to_sibling(u, n).wait_send()

            @pl.when(near)
            def _():
                to_partner(u, n).wait_send()

            @pl.when(jnp.logical_and(near, jnp.logical_or(n != node, u != unit)))
            def _():
                give_home(u, n).wait_send()

            return 0

        lax.fori_loop(0, nodes, each, 0)

        @pl.when(jnp.logical_not(near))
        def _():
            give_sum(u).wait_send()

        return 0

    lax.fori_loop(0, units, drained, 0)
    for j in range(max(units - 2, 0), units):
        give_half(j, 0).wait_send()


def on_device(tokens, route_ids, route_gates, limits, w_gate, w_up, w_down):
    nodes = lax.axis_size("node")
    locs = lax.axis_size("local")
    units = locs // 2
    hosted = nodes * (locs // GROUP)
    rows, width = tokens.shape
    slab = w_down.shape[1]
    piece = (width // COL // SPLIT) * COL
    assert width - SPLIT * piece == COL and SPLIT * CAP == SUB - 1
    assert CAP * COL <= piece and hosted <= 128
    xrows = -(-2 * nodes * CAP // SUB) * SUB
    block = (SUB, piece)
    dma = pltpu.SemaphoreType.DMA
    vmem = pl.BlockSpec(memory_space=pltpu.VMEM)
    hbm = pl.BlockSpec(memory_space=pl.ANY)
    return pl.pallas_call(
        functools.partial(kernel, (nodes, locs)),
        out_shape=jax.ShapeDtypeStruct((rows, width), BF),
        in_specs=[hbm, vmem, vmem, vmem, hbm, hbm, hbm],
        out_specs=vmem,
        scratch_shapes=[
            pltpu.VMEM((rows, width), BF),
            pltpu.VMEM((slab, width), BF),
            pltpu.VMEM((slab, width), BF),
            pltpu.VMEM((slab, width), BF),
            pltpu.VMEM((hosted,) + block, BF),
            pltpu.VMEM((units, 2, nodes) + block, BF),
            pltpu.VMEM((xrows, width), BF),
            pltpu.VMEM((units, nodes) + block, BF),
            pltpu.VMEM((2, nodes) + block, BF),
            pltpu.VMEM((units, nodes) + block, BF),
            pltpu.VMEM((units, nodes) + block, BF),
            pltpu.VMEM((hosted,) + block, BF),
            dma((4,)),
            dma((units, 2, nodes)),
            dma((hosted,)),
            dma((units, nodes)),
            dma((units, nodes)),
            dma((2,)),
            dma((units,)),
            dma((units,)),
            dma((units,)),
            dma((units, nodes)),
            dma((hosted,)),
        ],
        compiler_params=pltpu.CompilerParams(
            collective_id=0, has_side_effects=True, vmem_limit_bytes=60 * 1024 * 1024
        ),
        cost_estimate=pl.CostEstimate(
            flops=6 * locs * nodes * CAP * width * slab, bytes_accessed=6 * width * slab, transcendentals=0
        ),
    )(
        tokens,
        route_ids.T,
        route_gates.T,
        limits.reshape(1, -1),
        jnp.swapaxes(w_gate, 1, 2)[0],
        jnp.swapaxes(w_up, 1, 2)[0],
        w_down[0],
    )


def solution(mesh):
    return jax.shard_map(
        on_device,
        mesh=mesh,
        in_specs=(
            P(("node", "local"), None),
            P(("node", "local"), None),
            P(("node", "local"), None),
            P(),
            P(("node", "local"), None, None),
            P(("node", "local"), None, None),
            P(("node", "local"), None, None),
        ),
        out_specs=P(("node", "local"), None),
        check_vma=False,
    )
```

```python
import functools

import jax
import jax.numpy as jnp
from jax import lax
from jax.experimental import pallas as pl
from jax.experimental.pallas import tpu as pltpu
from jax.sharding import PartitionSpec as P

GROUP = 4
CAP = 5
PAIR = 2
SUB = 16
SPLIT = 3
COL = 256
BF = jnp.bfloat16
F32 = jnp.float32
MESH = pl.DeviceIdType.MESH


def dot(a, b):
    return jnp.dot(a, b, preferred_element_type=F32)


def dot_t(a, b):
    return lax.dot_general(a, b, (((1,), (1,)), ((), ())), preferred_element_type=F32)


def iota(shape, dim):
    return lax.broadcasted_iota(jnp.int32, shape, dim)


def div_cap(x):
    return (x * 205) >> 10


def kernel(
    dims,
    tok_hbm, ids_ref, gates_ref, limits_ref, wg_hbm, wu_hbm, wd_hbm,
    out_ref,
    tok, wg, wu, wd, pack, x, xu, own, sib, sib_in, par_in, home,
    in_sem, recv_x, send_d, send_s, send_r, send_p, recv_p, send_q, recv_q, send_h, recv_h,
):
    nodes, locs = dims
    groups = locs // GROUP
    units = locs // 2
    hosted = nodes * groups
    rows = tok.shape[0]
    width = tok.shape[1]
    piece = x.shape[-1]
    tail0 = SPLIT * piece
    cols = piece // COL
    packed = hosted * SUB
    srcs = PAIR * 2 * nodes
    steps = units // PAIR
    chunk = srcs * SUB
    xrows = xu.shape[0]

    node = lax.axis_index("node")
    loc = lax.axis_index("local")
    core = lax.rem(loc, 2)
    unit = loc // 2
    place = lax.rem(unit, 2)
    group = unit // 2
    sibling = (node, unit * 2 + (1 - core))
    partner = (node, group * GROUP + 2 * (1 - place) + core)

    loads = [
        pltpu.make_async_copy(tok_hbm, tok, in_sem.at[0]),
        pltpu.make_async_copy(wg_hbm, wg, in_sem.at[1]),
        pltpu.make_async_copy(wu_hbm, wu, in_sem.at[2]),
        pltpu.make_async_copy(wd_hbm, wd, in_sem.at[3]),
    ]
    loads[0].start()

    barrier = pltpu.get_barrier_semaphore()

    def greet(i, _):
        n, u = i // units, lax.rem(i, units)

        @pl.when(jnp.logical_or(n != node, u != unit))
        def _():
            pl.semaphore_signal(barrier, inc=1, device_id=(n, u * 2 + core), device_id_type=MESH)

        return 0

    lax.fori_loop(0, nodes * units, greet, 0)
    pl.semaphore_signal(barrier, inc=1, device_id=sibling, device_id_type=MESH)

    ep = 128
    expert = iota((ep, rows), 0)
    named = jnp.zeros((ep, rows), F32)
    gate = jnp.zeros((ep, rows), F32)
    for k in range(ids_ref.shape[0]):
        hit = ids_ref[k : k + 1, :] == expert
        named = named + jnp.where(hit, 1.0, 0.0)
        gate = gate + jnp.where(hit, gates_ref[k : k + 1, :].astype(F32), 0.0)
    earlier = jnp.where(iota((rows, rows), 0) < iota((rows, rows), 1), 1.0, 0.0).astype(BF)
    before = dot(named.astype(BF), earlier)
    lim = jnp.zeros((ep, rows), F32)
    for e in range(hosted):
        lim = jnp.where(expert == e, limits_ref[e].astype(F32), lim)
    kept = jnp.logical_and(named > 0.5, before < lim)
    slot = jnp.where(kept, before, -1.0)
    coef = jnp.where(kept, gate, 0.0)
    spread = jnp.where(iota((packed, ep), 0) // SUB == iota((packed, ep), 1), 1.0, 0.0).astype(BF)
    slot_m = dot(spread, slot.astype(BF))
    coef_m = dot(spread, coef.astype(BF))

    def member(line, slots, q):
        row = lax.rem(line, SUB)
        rank = (row * 11) >> 5
        ok = jnp.logical_and(row < SUB - 1, row - SPLIT * rank == q)
        return jnp.logical_and(ok, slots == rank.astype(F32))

    def member_tail(line, slots, r):
        return jnp.logical_and(lax.rem(line, SUB) == SUB - 1, slots == float(r))

    line = iota((packed, rows), 0)
    heads = [jnp.where(member(line, slot_m, q), 1.0, 0.0).astype(BF) for q in range(SPLIT)]
    tails = [jnp.where(member_tail(line, slot_m, r), 1.0, 0.0).astype(BF) for r in range(CAP)]

    loads[0].wait()
    for load in loads[1:]:
        load.start()
    for j in range(cols):
        acc = dot(heads[0], tok[:, j * COL : (j + 1) * COL])
        for q in range(1, SPLIT):
            acc = acc + dot(heads[q], tok[:, q * piece + j * COL : q * piece + (j + 1) * COL])
        if j < CAP:
            acc = acc + dot(tails[j], tok[:, tail0:])
        pack[:, :, j * COL : (j + 1) * COL] = acc.astype(BF).reshape(hosted, SUB, COL)

    pl.semaphore_wait(barrier, nodes * units)

    def near_place(src_group, src_place, g):
        return jnp.where(src_group < g, 0, jnp.where(src_group > g, 1, src_place))

    def target(i):
        g = lax.rem(group + lax.rem(i, groups), groups)
        n = lax.rem(node + i // groups, nodes)
        to_unit = 2 * g + near_place(group, place, g)
        e = n * groups + g
        return e, n, to_unit, jnp.logical_and(n == node, to_unit == unit)

    def dispatch(e, n, to_unit):
        return pltpu.make_async_remote_copy(
            src_ref=pack.at[e], dst_ref=x.at[unit, core, node], send_sem=send_d.at[e],
            recv_sem=recv_x.at[unit, core, node], device_id=(n, 2 * to_unit + core), device_id_type=MESH,
        )

    def send_out(i, _):
        e, n, to_unit, mine = target(i)

        @pl.when(mine)
        def _():
            pltpu.make_async_copy(pack.at[e], x.at[unit, core, node], recv_x.at[unit, core, node]).start()

        @pl.when(jnp.logical_not(mine))
        def _():
            dispatch(e, n, to_unit).start()

        return 0

    lax.fori_loop(0, hosted, send_out, 0)

    at_row, at_line = iota((xrows, chunk), 0), iota((xrows, chunk), 1)
    first = SUB * div_cap(at_row)
    rank = at_row - CAP * div_cap(at_row)
    open_all = jnp.concatenate(
        [jnp.where(at_line == first + SPLIT * rank + q, 1.0, 0.0).astype(BF) for q in range(SPLIT)], axis=0
    )
    open_tail = [
        jnp.where(jnp.logical_and(at_line == first + SUB - 1, rank == r), 1.0, 0.0).astype(BF) for r in range(CAP)
    ]
    at_line, at_row = iota((chunk, xrows), 0), iota((chunk, xrows), 1)
    blk = at_line // SUB
    half = blk // (PAIR * nodes)
    src = lax.rem(blk // nodes, PAIR) * (2 * nodes) + lax.rem(core + half, 2) * nodes + lax.rem(blk, nodes)
    sub_row = lax.rem(at_line, SUB)
    rank_of = at_row - CAP * div_cap(at_row)
    same = src == div_cap(at_row)
    close = [
        jnp.where(jnp.logical_and(same, sub_row == SPLIT * rank_of + q), 1.0, 0.0).astype(BF) for q in range(SPLIT)
    ]
    close_tail = [
        jnp.where(jnp.logical_and(same, jnp.logical_and(sub_row == SUB - 1, rank_of == r)), 1.0, 0.0).astype(BF)
        for r in range(CAP)
    ]

    def unit_at(j):
        return lax.rem(2 * group + PAIR * j, units)

    def is_near(u):
        return near_place(u // 2, lax.rem(u, 2), group) == place

    def to_sibling(u, n):
        return pltpu.make_async_remote_copy(
            src_ref=x.at[u, core, n], dst_ref=x.at[u, core, n], send_sem=send_s.at[u, n],
            recv_sem=recv_x.at[u, core, n], device_id=sibling, device_id_type=MESH,
        )

    def to_partner(u, n):
        return pltpu.make_async_remote_copy(
            src_ref=x.at[u, core, n], dst_ref=x.at[u, core, n], send_sem=send_r.at[u, n],
            recv_sem=recv_x.at[u, core, n], device_id=partner, device_id_type=MESH,
        )

    def give_half(j, k):
        b, u = lax.rem(j, 2), unit_at(j) + k
        return pltpu.make_async_remote_copy(
            src_ref=sib.at[b, k], dst_ref=sib_in.at[u], send_sem=send_p.at[b, k],
            recv_sem=recv_p.at[u], device_id=sibling, device_id_type=MESH,
        )

    def give_sum(u):
        return pltpu.make_async_remote_copy(
            src_ref=own.at[u], dst_ref=par_in.at[u], send_sem=send_q.at[u],
            recv_sem=recv_q.at[u], device_id=partner, device_id_type=MESH,
        )

    expert_here = node * groups + group

    def give_home(u, n):
        return pltpu.make_async_remote_copy(
            src_ref=own.at[u, n], dst_ref=home.at[expert_here], send_sem=send_h.at[u, n],
            recv_sem=recv_h.at[expert_here], device_id=(n, 2 * u + core), device_id_type=MESH,
        )

    def landed(ref, sem):
        pltpu.make_async_copy(ref, ref, sem).wait()

    def relay(j, k):
        u, n = unit_at(j) + k // nodes, lax.rem(node + nodes - lax.rem(k, nodes), nodes)
        landed(x.at[u, core, n], recv_x.at[u, core, n])

        @pl.when(is_near(u))
        def _():
            to_partner(u, n).start()

        to_sibling(u, n).start()

    def relay_next(j, ks):
        @pl.when(j + 1 < steps)
        def _():
            for k in ks:
                relay(j + 1, k)

    def add_core(j):
        for k in range(PAIR):
            v = unit_at(j) + k
            landed(sib_in.at[v], recv_p.at[v])

            @pl.when(jnp.logical_not(is_near(v)))
            def _():
                for n in range(nodes):
                    own[v, n] = (own[v, n].astype(F32) + sib_in[v, n].astype(F32)).astype(BF)
                give_sum(v).start()

    def add_chip(j):
        for k in range(PAIR):
            v = unit_at(j) + k

            @pl.when(is_near(v))
            def _():
                landed(par_in.at[v], recv_q.at[v])
                for n in range(nodes):
                    total = own[v, n].astype(F32) + sib_in[v, n].astype(F32) + par_in[v, n].astype(F32)
                    own[v, n] = total.astype(BF)
                    mine = jnp.logical_and(n == node, v == unit)

                    @pl.when(mine)
                    def _():
                        pltpu.make_async_copy(own.at[v, n], home.at[expert_here], recv_h.at[expert_here]).start()

                    @pl.when(jnp.logical_not(mine))
                    def _():
                        give_home(v, n).start()

    def step(j, _):
        u = unit_at(j)

        def arrive(i, _):
            v, n = u + i // nodes, lax.rem(i, nodes)
            landed(x.at[v, 1 - core, n], recv_x.at[v, 1 - core, n])
            return 0

        lax.fori_loop(0, PAIR * nodes, arrive, 0)
        tail = jnp.zeros((xrows, COL), F32)
        for c in range(cols):
            xc = x[pl.ds(u, PAIR), :, :, :, c * COL : (c + 1) * COL].reshape(chunk, COL)
            opened = dot(open_all, xc).astype(BF)
            for q in range(SPLIT):
                xu[:, q * piece + c * COL : q * piece + (c + 1) * COL] = opened[q * xrows : (q + 1) * xrows]
            if c < CAP:
                tail = tail + dot(open_tail[c], xc)
        xu[:, tail0:] = tail.astype(BF)

        relays = range(PAIR * nodes)
        relay_next(j, relays[:2])

        @pl.when(j == 0)
        def _():
            for load in loads[1:]:
                load.wait()

        act = dot_t(wg[...], xu[...])
        relay_next(j, relays[2:4])
        up = dot_t(wu[...], xu[...])
        hidden = (act / (1.0 + jnp.exp(-act)) * up).astype(BF)
        relay_next(j, relays[4:6])

        @pl.when(j >= 1)
        def _():
            add_core(j - 1)

        @pl.when(j >= 2)
        def _():
            for k in range(PAIR):
                give_half(j - 2, k).wait_send()

        spreads = [dot_t(m, hidden).astype(BF) for m in close]
        spread_tails = [dot_t(m, hidden).astype(BF) for m in close_tail]
        b = lax.rem(j, 2)
        for c in range(cols):
            acc = dot(spreads[0], wd[:, c * COL : (c + 1) * COL])
            for q in range(1, SPLIT):
                acc = acc + dot(spreads[q], wd[:, q * piece + c * COL : q * piece + (c + 1) * COL])
            if c < CAP:
                acc = acc + dot(spread_tails[c], wd[:, tail0:])
            parts = acc.astype(BF).reshape(2, PAIR, nodes, SUB, COL)
            own[pl.ds(u, PAIR), :, :, c * COL : (c + 1) * COL] = parts[0]
            sib[b, :, :, :, c * COL : (c + 1) * COL] = parts[1]
            if c == cols // 2:
                relay_next(j, relays[6:])
        for k in range(PAIR):
            give_half(j, k).start()

        @pl.when(j >= 1)
        def _():
            add_chip(j - 1)

        return 0

    def relay_first(k, _):
        relay(0, k)
        return 0

    lax.fori_loop(0, PAIR * nodes, relay_first, 0)
    lax.fori_loop(0, steps, step, 0)
    add_core(steps - 1)
    add_chip(steps - 1)

    line = iota((rows, packed), 1)
    slot_t = jnp.transpose(slot_m)
    coef_t = jnp.transpose(coef_m)
    heads = [jnp.where(member(line, slot_t, q), coef_t, 0.0).astype(BF) for q in range(SPLIT)]
    tails = [jnp.where(member_tail(line, slot_t, r), coef_t, 0.0).astype(BF) for r in range(CAP)]

    def returned(e, _):
        landed(home.at[e], recv_h.at[e])
        return 0

    lax.fori_loop(0, hosted, returned, 0)
    tail = jnp.zeros((rows, COL), F32)
    for c in range(cols):
        got = home[:, :, c * COL : (c + 1) * COL].reshape(packed, COL)
        for q in range(SPLIT):
            out_ref[:, q * piece + c * COL : q * piece + (c + 1) * COL] = dot(heads[q], got).astype(BF)
        if c < CAP:
            tail = tail + dot(tails[c], got)
    out_ref[:, tail0:] = tail.astype(BF)

    def sent(i, _):
        e, n, to_unit, mine = target(i)

        @pl.when(jnp.logical_not(mine))
        def _():
            dispatch(e, n, to_unit).wait_send()

        return 0

    lax.fori_loop(0, hosted, sent, 0)

    def drained(u, _):
        near = is_near(u)

        def each(n, _):
            to_sibling(u, n).wait_send()

            @pl.when(near)
            def _():
                to_partner(u, n).wait_send()

            @pl.when(jnp.logical_and(near, jnp.logical_or(n != node, u != unit)))
            def _():
                give_home(u, n).wait_send()

            return 0

        lax.fori_loop(0, nodes, each, 0)

        @pl.when(jnp.logical_not(near))
        def _():
            give_sum(u).wait_send()

        return 0

    lax.fori_loop(0, units, drained, 0)
    for j in range(max(steps - 2, 0), steps):
        for k in range(PAIR):
            give_half(j, k).wait_send()


def on_device(tokens, route_ids, route_gates, limits, w_gate, w_up, w_down):
    nodes = lax.axis_size("node")
    locs = lax.axis_size("local")
    units = locs // 2
    hosted = nodes * (locs // GROUP)
    rows, width = tokens.shape
    slab = w_down.shape[1]
    piece = (width // COL // SPLIT) * COL
    assert width - SPLIT * piece == COL and SPLIT * CAP == SUB - 1
    assert CAP * COL <= piece and hosted <= 128
    xrows = -(-PAIR * 2 * nodes * CAP // 128) * 128
    assert units % PAIR == 0 and GROUP == 2 * PAIR
    block = (SUB, piece)
    dma = pltpu.SemaphoreType.DMA
    vmem = pl.BlockSpec(memory_space=pltpu.VMEM)
    hbm = pl.BlockSpec(memory_space=pl.ANY)
    return pl.pallas_call(
        functools.partial(kernel, (nodes, locs)),
        out_shape=jax.ShapeDtypeStruct((rows, width), BF),
        in_specs=[hbm, vmem, vmem, pl.BlockSpec(memory_space=pltpu.SMEM), hbm, hbm, hbm],
        out_specs=vmem,
        scratch_shapes=[
            pltpu.VMEM((rows, width), BF),
            pltpu.VMEM((slab, width), BF),
            pltpu.VMEM((slab, width), BF),
            pltpu.VMEM((slab, width), BF),
            pltpu.VMEM((hosted,) + block, BF),
            pltpu.VMEM((units, 2, nodes) + block, BF),
            pltpu.VMEM((xrows, width), BF),
            pltpu.VMEM((units, nodes) + block, BF),
            pltpu.VMEM((2, PAIR, nodes) + block, BF),
            pltpu.VMEM((units, nodes) + block, BF),
            pltpu.VMEM((units, nodes) + block, BF),
            pltpu.VMEM((hosted,) + block, BF),
            dma((4,)),
            dma((units, 2, nodes)),
            dma((hosted,)),
            dma((units, nodes)),
            dma((units, nodes)),
            dma((2, PAIR)),
            dma((units,)),
            dma((units,)),
            dma((units,)),
            dma((units, nodes)),
            dma((hosted,)),
        ],
        compiler_params=pltpu.CompilerParams(
            collective_id=0, has_side_effects=True, vmem_limit_bytes=60 * 1024 * 1024
        ),
        cost_estimate=pl.CostEstimate(
            flops=6 * locs * nodes * CAP * width * slab, bytes_accessed=6 * width * slab, transcendentals=0
        ),
    )(
        tokens,
        route_ids.T,
        route_gates.T,
        limits,
        jnp.swapaxes(w_gate, 1, 2)[0],
        jnp.swapaxes(w_up, 1, 2)[0],
        w_down[0],
    )


def solution(mesh):
    return jax.shard_map(
        on_device,
        mesh=mesh,
        in_specs=(
            P(("node", "local"), None),
            P(("node", "local"), None),
            P(("node", "local"), None),
            P(),
            P(("node", "local"), None, None),
            P(("node", "local"), None, None),
            P(("node", "local"), None, None),
        ),
        out_specs=P(("node", "local"), None),
        check_vma=False,
    )
```

```python
import functools

import jax
import jax.numpy as jnp
from jax import lax
from jax.experimental import pallas as pl
from jax.experimental.pallas import tpu as pltpu
from jax.sharding import PartitionSpec as P

GROUP = 4
CAP = 5
PIECES = 3
UNIT_ROWS = 48
SUB = 16
SPLIT = 3
COL = 256
BF = jnp.bfloat16
F32 = jnp.float32
MESH = pl.DeviceIdType.MESH


def dot(a, b):
    return jnp.dot(a, b, preferred_element_type=F32)


def dot_t(a, b):
    return lax.dot_general(a, b, (((1,), (1,)), ((), ())), preferred_element_type=F32)


def iota(shape, dim):
    return lax.broadcasted_iota(jnp.int32, shape, dim)


def div_cap(x):
    return (x * 205) >> 10


def kernel(
    dims,
    tok_hbm, ids_ref, gates_ref, limits_ref, wg_hbm, wu_hbm, wd_hbm,
    out_hbm,
    tok, wg, wu, wd, pack, x, xu, xt, act, up, own, sib, sib_in, par_in, home,
    in_sem, recv_x, recv_g, send_d, send_s, send_r, send_p, recv_p, send_q, recv_q, send_h, recv_h,
):
    nodes, locs = dims
    groups = locs // GROUP
    units = locs // 2
    hosted = nodes * groups
    rows = tok.shape[0]
    pieces, part = x.shape[0], x.shape[-1]
    piece = pieces * part
    tail0 = SPLIT * piece
    cols = part // COL
    packed = hosted * SUB
    chunk = 2 * nodes * SUB
    xrows = xu.shape[0]

    node = lax.axis_index("node")
    loc = lax.axis_index("local")
    core = lax.rem(loc, 2)
    unit = loc // 2
    place = lax.rem(unit, 2)
    group = unit // 2
    sibling = (node, unit * 2 + (1 - core))
    partner = (node, group * GROUP + 2 * (1 - place) + core)

    loads = [
        pltpu.make_async_copy(tok_hbm, tok, in_sem.at[0]),
        pltpu.make_async_copy(wg_hbm, wg, in_sem.at[1]),
        pltpu.make_async_copy(wu_hbm, wu, in_sem.at[2]),
        pltpu.make_async_copy(wd_hbm, wd, in_sem.at[3]),
    ]
    loads[0].start()

    barrier = pltpu.get_barrier_semaphore()

    def greet(i, _):
        n, u = i // units, lax.rem(i, units)

        @pl.when(jnp.logical_or(n != node, u != unit))
        def _():
            pl.semaphore_signal(barrier, inc=1, device_id=(n, u * 2 + core), device_id_type=MESH)

        return 0

    lax.fori_loop(0, nodes * units, greet, 0)
    pl.semaphore_signal(barrier, inc=1, device_id=sibling, device_id_type=MESH)

    ep = 128
    expert = iota((ep, rows), 0)
    named = jnp.zeros((ep, rows), F32)
    gate = jnp.zeros((ep, rows), F32)
    for k in range(ids_ref.shape[0]):
        hit = ids_ref[k : k + 1, :] == expert
        named = named + jnp.where(hit, 1.0, 0.0)
        gate = gate + jnp.where(hit, gates_ref[k : k + 1, :].astype(F32), 0.0)
    earlier = jnp.where(iota((rows, rows), 0) < iota((rows, rows), 1), 1.0, 0.0).astype(BF)
    before = dot(named.astype(BF), earlier)
    lim = jnp.zeros((ep, rows), F32)
    for e in range(hosted):
        lim = jnp.where(expert == e, limits_ref[e].astype(F32), lim)
    kept = jnp.logical_and(named > 0.5, before < lim)
    slot = jnp.where(kept, before, -1.0)
    coef = jnp.where(kept, gate, 0.0)
    spread = jnp.where(iota((packed, ep), 0) // SUB == iota((packed, ep), 1), 1.0, 0.0).astype(BF)
    slot_m = dot(spread, slot.astype(BF))
    coef_m = dot(spread, coef.astype(BF))

    def member(line, slots, q):
        row = lax.rem(line, SUB)
        rank = (row * 11) >> 5
        ok = jnp.logical_and(row < SUB - 1, row - SPLIT * rank == q)
        return jnp.logical_and(ok, slots == rank.astype(F32))

    def member_tail(line, slots, r):
        return jnp.logical_and(lax.rem(line, SUB) == SUB - 1, slots == float(r))

    line = iota((packed, rows), 0)
    heads = [jnp.where(member(line, slot_m, q), 1.0, 0.0).astype(BF) for q in range(SPLIT)]
    tails = [jnp.where(member_tail(line, slot_m, r), 1.0, 0.0).astype(BF) for r in range(CAP)]

    loads[0].wait()
    for load in loads[1:]:
        load.start()

    def near_place(src_group, src_place, g):
        return jnp.where(src_group < g, 0, jnp.where(src_group > g, 1, src_place))

    def target(i):
        g = lax.rem(group + lax.rem(i, groups), groups)
        n = lax.rem(node + i // groups, nodes)
        to_unit = 2 * g + near_place(group, place, g)
        e = n * groups + g
        return e, n, to_unit, jnp.logical_and(n == node, to_unit == unit)

    def dispatch(p, e, n, to_unit):
        return pltpu.make_async_remote_copy(
            src_ref=pack.at[p, e], dst_ref=x.at[p, unit, core, node], send_sem=send_d.at[p, e],
            recv_sem=recv_x.at[p, unit, node], device_id=(n, 2 * to_unit + core), device_id_type=MESH,
        )

    for p in range(pieces):
        for c in range(cols):
            j = p * cols + c
            acc = dot(heads[0], tok[:, j * COL : (j + 1) * COL])
            for q in range(1, SPLIT):
                acc = acc + dot(heads[q], tok[:, q * piece + j * COL : q * piece + (j + 1) * COL])
            if j < CAP:
                acc = acc + dot(tails[j], tok[:, tail0:])
            pack[p, :, :, c * COL : (c + 1) * COL] = acc.astype(BF).reshape(hosted, SUB, COL)
        if p == 0:
            pl.semaphore_wait(barrier, nodes * units)

        def send_out(i, _):
            e, n, to_unit, mine = target(i)

            @pl.when(mine)
            def _():
                pltpu.make_async_copy(pack.at[p, e], x.at[p, unit, core, node], recv_x.at[p, unit, node]).start()

            @pl.when(jnp.logical_not(mine))
            def _():
                dispatch(p, e, n, to_unit).start()

            return 0

        lax.fori_loop(0, hosted, send_out, 0)

    def opener(parts):
        i, m = iota((UNIT_ROWS, chunk), 0), iota((UNIT_ROWS, chunk), 1)
        first, rank = SUB * div_cap(i), i - CAP * div_cap(i)
        out = [m == first + SPLIT * rank + q for q in range(SPLIT)]
        out += [jnp.logical_and(m == first + SUB - 1, rank == r) for r in parts]
        return jnp.concatenate([jnp.where(o, 1.0, 0.0) for o in out], axis=0).astype(BF)

    def closer(parts):
        m, i = iota((chunk, UNIT_ROWS), 0), iota((chunk, UNIT_ROWS), 1)
        blk, sub_row, rank = m // SUB, lax.rem(m, SUB), i - CAP * div_cap(i)
        src = lax.rem(core + blk // nodes, 2) * nodes + lax.rem(blk, nodes)
        same = src == div_cap(i)
        out = [jnp.logical_and(same, sub_row == SPLIT * rank + q) for q in range(SPLIT)]
        out += [jnp.logical_and(same, jnp.logical_and(sub_row == SUB - 1, rank == r)) for r in parts]
        return jnp.concatenate([jnp.where(o, 1.0, 0.0) for o in out], axis=1).astype(BF)

    tail_parts = [[j] if j < CAP else [] for j in range(pieces * cols)]

    def is_near(u):
        return near_place(u // 2, lax.rem(u, 2), group) == place

    def to_sibling(p, u):
        return pltpu.make_async_remote_copy(
            src_ref=x.at[p, u, core], dst_ref=x.at[p, u, core], send_sem=send_s.at[p, u],
            recv_sem=recv_g.at[p, u, core], device_id=sibling, device_id_type=MESH,
        )

    def to_partner(p, u):
        return pltpu.make_async_remote_copy(
            src_ref=x.at[p, u, core], dst_ref=x.at[p, u, core], send_sem=send_r.at[p, u],
            recv_sem=recv_g.at[p, u, core], device_id=partner, device_id_type=MESH,
        )

    def give_half(p):
        return pltpu.make_async_remote_copy(
            src_ref=sib.at[p], dst_ref=sib_in.at[p], send_sem=send_p.at[p],
            recv_sem=recv_p.at[p], device_id=sibling, device_id_type=MESH,
        )

    def give_sum(p, u):
        return pltpu.make_async_remote_copy(
            src_ref=own.at[p, u], dst_ref=par_in.at[p, u], send_sem=send_q.at[p, u],
            recv_sem=recv_q.at[p, u], device_id=partner, device_id_type=MESH,
        )

    expert_here = node * groups + group

    def give_home(p, u, n):
        return pltpu.make_async_remote_copy(
            src_ref=own.at[p, u, n], dst_ref=home.at[p, expert_here], send_sem=send_h.at[p, u, n],
            recv_sem=recv_h.at[p, expert_here], device_id=(n, 2 * u + core), device_id_type=MESH,
        )

    def landed(ref, sem):
        pltpu.make_async_copy(ref, ref, sem).wait()

    def relay(p):
        def first(k, _):
            u = lax.rem(2 * group + k, units)

            @pl.when(is_near(u))
            def _():
                for n in range(nodes):
                    landed(x.at[p, u, core, n], recv_x.at[p, u, n])
                to_partner(p, u).start()
                to_sibling(p, u).start()

            return 0

        def second(k, _):
            u = lax.rem(2 * group + k, units)

            @pl.when(jnp.logical_not(is_near(u)))
            def _():
                landed(x.at[p, u, core], recv_g.at[p, u, core])
                to_sibling(p, u).start()

            return 0

        def third(k, _):
            u = lax.rem(2 * group + k, units)
            landed(x.at[p, u, 1 - core], recv_g.at[p, u, 1 - core])
            return 0

        lax.fori_loop(0, units, first, 0)
        lax.fori_loop(0, units, second, 0)
        lax.fori_loop(0, units, third, 0)

    if xrows > units * UNIT_ROWS:
        spare = (xrows - units * UNIT_ROWS, xu.shape[1])
        xu[units * UNIT_ROWS :, :] = jnp.zeros(spare, BF)
        xt[units * UNIT_ROWS :, :] = jnp.zeros((spare[0], COL), BF)
    last_tail = (CAP - 1) // cols
    for p in range(pieces):
        relay(p)
        for c in range(cols):
            j = p * cols + c
            opening = opener(tail_parts[j])

            def unpack(u, _):
                base = pl.multiple_of(u * UNIT_ROWS, SUB)
                xc = x[p, u, :, :, :, c * COL : (c + 1) * COL].reshape(chunk, COL)
                opened = dot(opening, xc).astype(BF)
                for q in range(SPLIT):
                    xu[pl.ds(base, UNIT_ROWS), q * part + c * COL : q * part + (c + 1) * COL] = opened[
                        q * UNIT_ROWS : (q + 1) * UNIT_ROWS
                    ]
                if j < CAP:
                    more = opened[SPLIT * UNIT_ROWS :]
                    if j > 0:
                        more = xt[pl.ds(base, UNIT_ROWS), :] + more
                    xt[pl.ds(base, UNIT_ROWS), :] = more
                return 0

            lax.fori_loop(0, units, unpack, 0, unroll=True if units <= 4 else 1)
        if p == 0:
            for load in loads[1:]:
                load.wait()
        for w, total in ((wg, act), (wu, up)):
            acc = dot_t(w[:, p * part : (p + 1) * part], xu[:, :part])
            for q in range(1, SPLIT):
                at = q * piece + p * part
                acc = acc + dot_t(w[:, at : at + part], xu[:, q * part : (q + 1) * part])
            if p == last_tail:
                acc = acc + dot_t(w[:, tail0:], xt[...])
            total[...] = acc if p == 0 else total[...] + acc

    hidden_t = (act[...] / (1.0 + jnp.exp(-act[...])) * up[...]).astype(BF)
    eye = jnp.where(iota((xrows, xrows), 0) == iota((xrows, xrows), 1), 1.0, 0.0).astype(BF)
    hidden = dot_t(eye, hidden_t).astype(BF)
    last = dot(hidden, wd[:, tail0:]).astype(BF)

    def add_core(p):
        landed(sib_in.at[p], recv_p.at[p])

        def far(u, _):
            @pl.when(jnp.logical_not(is_near(u)))
            def _():
                for n in range(nodes):
                    own[p, u, n] = (own[p, u, n].astype(F32) + sib_in[p, u, n].astype(F32)).astype(BF)
                give_sum(p, u).start()

            return 0

        lax.fori_loop(0, units, far, 0)

    def add_chip(p):
        def near(u, _):
            @pl.when(is_near(u))
            def _():
                landed(par_in.at[p, u], recv_q.at[p, u])
                for n in range(nodes):
                    total = own[p, u, n].astype(F32) + sib_in[p, u, n].astype(F32) + par_in[p, u, n].astype(F32)
                    own[p, u, n] = total.astype(BF)
                    mine = jnp.logical_and(n == node, u == unit)

                    @pl.when(mine)
                    def _():
                        pltpu.make_async_copy(
                            own.at[p, u, n], home.at[p, expert_here], recv_h.at[p, expert_here]
                        ).start()

                    @pl.when(jnp.logical_not(mine))
                    def _():
                        give_home(p, u, n).start()

            return 0

        lax.fori_loop(0, units, near, 0)

    for p in range(pieces):
        for c in range(cols):
            j = p * cols + c
            outs = [
                dot(hidden, wd[:, q * piece + j * COL : q * piece + (j + 1) * COL]).astype(BF) for q in range(SPLIT)
            ]
            if j < CAP:
                outs.append(last)
            closing = closer(tail_parts[j])
            for u in range(units):
                mine = [o[u * UNIT_ROWS : (u + 1) * UNIT_ROWS] for o in outs]
                halves = dot(closing, jnp.concatenate(mine, axis=0)).astype(BF).reshape(2, nodes, SUB, COL)
                own[p, u, :, :, c * COL : (c + 1) * COL] = halves[0]
                sib[p, u, :, :, c * COL : (c + 1) * COL] = halves[1]
        give_half(p).start()
        if p >= 1:
            add_core(p - 1)
        if p >= 2:
            add_chip(p - 2)
    add_core(pieces - 1)
    for p in range(max(pieces - 2, 0), pieces):
        add_chip(p)

    line = iota((rows, packed), 1)
    slot_t = jnp.transpose(slot_m)
    coef_t = jnp.transpose(coef_m)
    heads = [jnp.where(member(line, slot_t, q), coef_t, 0.0).astype(BF) for q in range(SPLIT)]
    tails = [jnp.where(member_tail(line, slot_t, r), coef_t, 0.0).astype(BF) for r in range(CAP)]
    tail = jnp.zeros((rows, COL), F32)
    for p in range(pieces):
        def returned(e, _):
            landed(home.at[p, e], recv_h.at[p, e])
            return 0

        lax.fori_loop(0, hosted, returned, 0)
        for c in range(cols):
            j = p * cols + c
            got = home[p, :, :, c * COL : (c + 1) * COL].reshape(packed, COL)
            for q in range(SPLIT):
                tok[:, q * piece + j * COL : q * piece + (j + 1) * COL] = dot(heads[q], got).astype(BF)
            if j < CAP:
                tail = tail + dot(tails[j], got)
    tok[:, tail0:] = tail.astype(BF)
    store = pltpu.make_async_copy(tok, out_hbm, in_sem.at[0])
    store.start()

    for p in range(pieces):
        def sent(i, _):
            e, n, to_unit, mine = target(i)

            @pl.when(jnp.logical_not(mine))
            def _():
                dispatch(p, e, n, to_unit).wait_send()

            return 0

        lax.fori_loop(0, hosted, sent, 0)

        def drained(u, _):
            near = is_near(u)
            to_sibling(p, u).wait_send()

            @pl.when(near)
            def _():
                to_partner(p, u).wait_send()
                for n in range(nodes):
                    @pl.when(jnp.logical_or(n != node, u != unit))
                    def _():
                        give_home(p, u, n).wait_send()

            @pl.when(jnp.logical_not(near))
            def _():
                give_sum(p, u).wait_send()

            return 0

        lax.fori_loop(0, units, drained, 0)
        give_half(p).wait_send()
    store.wait()


def on_device(tokens, route_ids, route_gates, limits, w_gate, w_up, w_down):
    nodes = lax.axis_size("node")
    locs = lax.axis_size("local")
    units = locs // 2
    hosted = nodes * (locs // GROUP)
    rows, width = tokens.shape
    slab = w_down.shape[1]
    piece = (width // COL // SPLIT) * COL
    part = piece // PIECES
    assert width - SPLIT * piece == COL and SPLIT * CAP == SUB - 1 and part * PIECES == piece and part % COL == 0
    assert CAP * COL <= piece and hosted <= 128 and 2 * nodes * CAP <= UNIT_ROWS
    xrows = -(-units * UNIT_ROWS // 128) * 128
    block = (SUB, part)
    dma = pltpu.SemaphoreType.DMA
    vmem = pl.BlockSpec(memory_space=pltpu.VMEM)
    hbm = pl.BlockSpec(memory_space=pl.ANY)
    return pl.pallas_call(
        functools.partial(kernel, (nodes, locs)),
        out_shape=jax.ShapeDtypeStruct((rows, width), BF),
        in_specs=[hbm, vmem, vmem, pl.BlockSpec(memory_space=pltpu.SMEM), hbm, hbm, hbm],
        out_specs=hbm,
        scratch_shapes=[
            pltpu.VMEM((rows, width), BF),
            pltpu.VMEM((slab, width), BF),
            pltpu.VMEM((slab, width), BF),
            pltpu.VMEM((slab, width), BF),
            pltpu.VMEM((PIECES, hosted) + block, BF),
            pltpu.VMEM((PIECES, units, 2, nodes) + block, BF),
            pltpu.VMEM((xrows, SPLIT * part), BF),
            pltpu.VMEM((xrows, COL), BF),
            pltpu.VMEM((slab, xrows), F32),
            pltpu.VMEM((slab, xrows), F32),
            pltpu.VMEM((PIECES, units, nodes) + block, BF),
            pltpu.VMEM((PIECES, units, nodes) + block, BF),
            pltpu.VMEM((PIECES, units, nodes) + block, BF),
            pltpu.VMEM((PIECES, units, nodes) + block, BF),
            pltpu.VMEM((PIECES, hosted) + block, BF),
            dma((4,)),
            dma((PIECES, units, nodes)),
            dma((PIECES, units, 2)),
            dma((PIECES, hosted)),
            dma((PIECES, units)),
            dma((PIECES, units)),
            dma((PIECES,)),
            dma((PIECES,)),
            dma((PIECES, units)),
            dma((PIECES, units)),
            dma((PIECES, units, nodes)),
            dma((PIECES, hosted)),
        ],
        compiler_params=pltpu.CompilerParams(
            collective_id=0, has_side_effects=True, vmem_limit_bytes=62 * 1024 * 1024
        ),
        cost_estimate=pl.CostEstimate(
            flops=6 * locs * nodes * CAP * width * slab, bytes_accessed=6 * width * slab, transcendentals=0
        ),
    )(
        tokens,
        route_ids.T,
        route_gates.T,
        limits,
        jnp.swapaxes(w_gate, 1, 2)[0],
        jnp.swapaxes(w_up, 1, 2)[0],
        w_down[0],
    )


def solution(mesh):
    return jax.shard_map(
        on_device,
        mesh=mesh,
        in_specs=(
            P(("node", "local"), None),
            P(("node", "local"), None),
            P(("node", "local"), None),
            P(),
            P(("node", "local"), None, None),
            P(("node", "local"), None, None),
            P(("node", "local"), None, None),
        ),
        out_specs=P(("node", "local"), None),
        check_vma=False,
    )
```

```python
import functools

import jax
import jax.numpy as jnp
from jax import lax
from jax.experimental import pallas as pl
from jax.experimental.pallas import tpu as pltpu
from jax.sharding import PartitionSpec as P

GROUP = 4
CAP = 5
PIECES = 3
UNIT_ROWS = 48
SUB = 16
SPLIT = 3
COL = 256
BF = jnp.bfloat16
F32 = jnp.float32
MESH = pl.DeviceIdType.MESH


def dot(a, b):
    return jnp.dot(a, b, preferred_element_type=F32)


def dot_t(a, b):
    return lax.dot_general(a, b, (((1,), (1,)), ((), ())), preferred_element_type=F32)


def iota(shape, dim):
    return lax.broadcasted_iota(jnp.int32, shape, dim)


def div_cap(x):
    return (x * 205) >> 10


def kernel(
    dims,
    tok_hbm, ids_ref, gates_ref, limits_ref, wg_hbm, wu_hbm, wd_hbm,
    out_hbm,
    tok, wgu, wd, pack, x, xu, xt, both, own, sib, sib_in, par_in, home,
    in_sem, recv_x, recv_g, send_d, send_s, send_r, send_p, recv_p, send_q, recv_q, send_h, recv_h,
):
    nodes, locs = dims
    groups = locs // GROUP
    units = locs // 2
    hosted = nodes * groups
    rows = tok.shape[0]
    pieces, part = x.shape[0], x.shape[-1]
    piece = pieces * part
    tail0 = SPLIT * piece
    cols = part // COL
    packed = hosted * SUB
    chunk = 2 * nodes * SUB
    xrows = xu.shape[0]
    slab = wd.shape[0]

    node = lax.axis_index("node")
    loc = lax.axis_index("local")
    core = lax.rem(loc, 2)
    unit = loc // 2
    place = lax.rem(unit, 2)
    group = unit // 2
    sibling = (node, unit * 2 + (1 - core))
    partner = (node, group * GROUP + 2 * (1 - place) + core)

    loads = [
        pltpu.make_async_copy(tok_hbm, tok, in_sem.at[0]),
        pltpu.make_async_copy(wg_hbm, wgu.at[pl.ds(0, slab)], in_sem.at[1]),
        pltpu.make_async_copy(wu_hbm, wgu.at[pl.ds(slab, slab)], in_sem.at[2]),
        pltpu.make_async_copy(wd_hbm, wd, in_sem.at[3]),
    ]
    loads[0].start()

    barrier = pltpu.get_barrier_semaphore()

    def greet(i, _):
        n, u = i // units, lax.rem(i, units)

        @pl.when(jnp.logical_or(n != node, u != unit))
        def _():
            pl.semaphore_signal(barrier, inc=1, device_id=(n, u * 2 + core), device_id_type=MESH)

        return 0

    lax.fori_loop(0, nodes * units, greet, 0)
    pl.semaphore_signal(barrier, inc=1, device_id=sibling, device_id_type=MESH)

    ep = 128
    expert = iota((ep, rows), 0)
    named = jnp.zeros((ep, rows), F32)
    gate = jnp.zeros((ep, rows), F32)
    for k in range(ids_ref.shape[0]):
        hit = ids_ref[k : k + 1, :] == expert
        named = named + jnp.where(hit, 1.0, 0.0)
        gate = gate + jnp.where(hit, gates_ref[k : k + 1, :].astype(F32), 0.0)
    earlier = jnp.where(iota((rows, rows), 0) < iota((rows, rows), 1), 1.0, 0.0).astype(BF)
    before = dot(named.astype(BF), earlier)
    lim = jnp.zeros((ep, rows), F32)
    for e in range(hosted):
        lim = jnp.where(expert == e, limits_ref[e].astype(F32), lim)
    kept = jnp.logical_and(named > 0.5, before < lim)
    slot = jnp.where(kept, before, -1.0)
    coef = jnp.where(kept, gate, 0.0)
    spread = jnp.where(iota((packed, ep), 0) // SUB == iota((packed, ep), 1), 1.0, 0.0).astype(BF)
    slot_m = dot(spread, slot.astype(BF))
    coef_m = dot(spread, coef.astype(BF))

    def member(line, slots, q):
        row = lax.rem(line, SUB)
        rank = (row * 11) >> 5
        ok = jnp.logical_and(row < SUB - 1, row - SPLIT * rank == q)
        return jnp.logical_and(ok, slots == rank.astype(F32))

    def member_tail(line, slots, r):
        return jnp.logical_and(lax.rem(line, SUB) == SUB - 1, slots == float(r))

    line = iota((packed, rows), 0)
    heads = [jnp.where(member(line, slot_m, q), 1.0, 0.0).astype(BF) for q in range(SPLIT)]
    tails = [jnp.where(member_tail(line, slot_m, r), 1.0, 0.0).astype(BF) for r in range(CAP)]

    loads[0].wait()
    for load in loads[1:]:
        load.start()

    def near_place(src_group, src_place, g):
        return jnp.where(src_group < g, 0, jnp.where(src_group > g, 1, src_place))

    def target(i):
        g = lax.rem(group + lax.rem(i, groups), groups)
        n = lax.rem(node + i // groups, nodes)
        to_unit = 2 * g + near_place(group, place, g)
        e = n * groups + g
        return e, n, to_unit, jnp.logical_and(n == node, to_unit == unit)

    def dispatch(p, e, n, to_unit):
        return pltpu.make_async_remote_copy(
            src_ref=pack.at[p, e], dst_ref=x.at[p, unit, core, node], send_sem=send_d.at[p, e],
            recv_sem=recv_x.at[p, unit, node], device_id=(n, 2 * to_unit + core), device_id_type=MESH,
        )

    for p in range(pieces):
        for c in range(cols):
            j = p * cols + c
            acc = dot(heads[0], tok[:, j * COL : (j + 1) * COL])
            for q in range(1, SPLIT):
                acc = acc + dot(heads[q], tok[:, q * piece + j * COL : q * piece + (j + 1) * COL])
            if j < CAP:
                acc = acc + dot(tails[j], tok[:, tail0:])
            pack[p, :, :, c * COL : (c + 1) * COL] = acc.astype(BF).reshape(hosted, SUB, COL)
        if p == 0:
            pl.semaphore_wait(barrier, nodes * units)

        def send_out(i, _):
            e, n, to_unit, mine = target(i)

            @pl.when(mine)
            def _():
                pltpu.make_async_copy(pack.at[p, e], x.at[p, unit, core, node], recv_x.at[p, unit, node]).start()

            @pl.when(jnp.logical_not(mine))
            def _():
                dispatch(p, e, n, to_unit).start()

            return 0

        lax.fori_loop(0, hosted, send_out, 0)

    def opener(parts):
        i, m = iota((UNIT_ROWS, chunk), 0), iota((UNIT_ROWS, chunk), 1)
        first, rank = SUB * div_cap(i), i - CAP * div_cap(i)
        out = [m == first + SPLIT * rank + q for q in range(SPLIT)]
        out += [jnp.logical_and(m == first + SUB - 1, rank == r) for r in parts]
        return jnp.concatenate([jnp.where(o, 1.0, 0.0) for o in out], axis=0).astype(BF)

    def closer(parts):
        m, i = iota((chunk, UNIT_ROWS), 0), iota((chunk, UNIT_ROWS), 1)
        blk, sub_row, rank = m // SUB, lax.rem(m, SUB), i - CAP * div_cap(i)
        src = lax.rem(core + blk // nodes, 2) * nodes + lax.rem(blk, nodes)
        same = src == div_cap(i)
        out = [jnp.logical_and(same, sub_row == SPLIT * rank + q) for q in range(SPLIT)]
        out += [jnp.logical_and(same, jnp.logical_and(sub_row == SUB - 1, rank == r)) for r in parts]
        return jnp.concatenate([jnp.where(o, 1.0, 0.0) for o in out], axis=1).astype(BF)

    tail_parts = [[j] if j < CAP else [] for j in range(pieces * cols)]

    def is_near(u):
        return near_place(u // 2, lax.rem(u, 2), group) == place

    def to_sibling(p, u):
        return pltpu.make_async_remote_copy(
            src_ref=x.at[p, u, core], dst_ref=x.at[p, u, core], send_sem=send_s.at[p, u],
            recv_sem=recv_g.at[p, u, core], device_id=sibling, device_id_type=MESH,
        )

    def to_partner(p, u):
        return pltpu.make_async_remote_copy(
            src_ref=x.at[p, u, core], dst_ref=x.at[p, u, core], send_sem=send_r.at[p, u],
            recv_sem=recv_g.at[p, u, core], device_id=partner, device_id_type=MESH,
        )

    def give_half(p):
        return pltpu.make_async_remote_copy(
            src_ref=sib.at[p], dst_ref=sib_in.at[p], send_sem=send_p.at[p],
            recv_sem=recv_p.at[p], device_id=sibling, device_id_type=MESH,
        )

    def give_sum(p, u):
        return pltpu.make_async_remote_copy(
            src_ref=own.at[p, u], dst_ref=par_in.at[p, u], send_sem=send_q.at[p, u],
            recv_sem=recv_q.at[p, u], device_id=partner, device_id_type=MESH,
        )

    expert_here = node * groups + group

    def give_home(p, u, n):
        return pltpu.make_async_remote_copy(
            src_ref=own.at[p, u, n], dst_ref=home.at[p, expert_here], send_sem=send_h.at[p, u, n],
            recv_sem=recv_h.at[p, expert_here], device_id=(n, 2 * u + core), device_id_type=MESH,
        )

    def landed(ref, sem):
        pltpu.make_async_copy(ref, ref, sem).wait()

    def relay_near(p):
        def first(k, _):
            u = lax.rem(2 * group + k, units)

            @pl.when(is_near(u))
            def _():
                for n in range(nodes):
                    landed(x.at[p, u, core, n], recv_x.at[p, u, n])
                to_partner(p, u).start()
                to_sibling(p, u).start()

            return 0

        lax.fori_loop(0, units, first, 0)

    def relay_far(p):
        def second(k, _):
            u = lax.rem(2 * group + k, units)

            @pl.when(jnp.logical_not(is_near(u)))
            def _():
                landed(x.at[p, u, core], recv_g.at[p, u, core])
                to_sibling(p, u).start()

            return 0

        def third(k, _):
            u = lax.rem(2 * group + k, units)
            landed(x.at[p, u, 1 - core], recv_g.at[p, u, 1 - core])
            return 0

        lax.fori_loop(0, units, second, 0)
        lax.fori_loop(0, units, third, 0)

    if xrows > units * UNIT_ROWS:
        spare = (xrows - units * UNIT_ROWS, xu.shape[1])
        xu[units * UNIT_ROWS :, :] = jnp.zeros(spare, BF)
        xt[units * UNIT_ROWS :, :] = jnp.zeros((spare[0], COL), BF)
    last_tail = (CAP - 1) // cols
    relay_near(0)
    for p in range(pieces):
        relay_far(p)
        for c in range(cols):
            j = p * cols + c
            opening = opener(tail_parts[j])

            def unpack(u, _):
                base = pl.multiple_of(u * UNIT_ROWS, SUB)
                xc = x[p, u, :, :, :, c * COL : (c + 1) * COL].reshape(chunk, COL)
                opened = dot(opening, xc).astype(BF)
                for q in range(SPLIT):
                    xu[pl.ds(base, UNIT_ROWS), q * part + c * COL : q * part + (c + 1) * COL] = opened[
                        q * UNIT_ROWS : (q + 1) * UNIT_ROWS
                    ]
                if j < CAP:
                    more = opened[SPLIT * UNIT_ROWS :]
                    if j > 0:
                        more = xt[pl.ds(base, UNIT_ROWS), :] + more
                    xt[pl.ds(base, UNIT_ROWS), :] = more
                return 0

            lax.fori_loop(0, units, unpack, 0, unroll=True if units <= 4 else 1)
        if p == 0:
            for load in loads[1:]:
                load.wait()
        acc = dot_t(wgu[:, p * part : (p + 1) * part], xu[:, :part])
        both[...] = acc if p == 0 else both[...] + acc
        if p + 1 < pieces:
            relay_near(p + 1)
        acc = dot_t(wgu[:, piece + p * part : piece + (p + 1) * part], xu[:, part : 2 * part])
        for q in range(2, SPLIT):
            at = q * piece + p * part
            acc = acc + dot_t(wgu[:, at : at + part], xu[:, q * part : (q + 1) * part])
        if p == last_tail:
            acc = acc + dot_t(wgu[:, tail0:], xt[...])
        both[...] = both[...] + acc

    act, up = both[:slab], both[slab:]
    hidden_t = (act / (1.0 + jnp.exp(-act)) * up).astype(BF)
    filled = (units * UNIT_ROWS, xrows)
    eye = jnp.where(iota(filled, 0) == iota(filled, 1), 1.0, 0.0).astype(BF)
    hidden = dot_t(eye, hidden_t).astype(BF)
    last = dot(hidden, wd[:, tail0:]).astype(BF)

    def add_core(p):
        landed(sib_in.at[p], recv_p.at[p])

        def far(u, _):
            @pl.when(jnp.logical_not(is_near(u)))
            def _():
                for n in range(nodes):
                    own[p, u, n] = (own[p, u, n].astype(F32) + sib_in[p, u, n].astype(F32)).astype(BF)
                give_sum(p, u).start()

            return 0

        lax.fori_loop(0, units, far, 0)

    def add_chip(p):
        def near(u, _):
            @pl.when(is_near(u))
            def _():
                landed(par_in.at[p, u], recv_q.at[p, u])
                for n in range(nodes):
                    total = own[p, u, n].astype(F32) + sib_in[p, u, n].astype(F32) + par_in[p, u, n].astype(F32)
                    own[p, u, n] = total.astype(BF)
                    mine = jnp.logical_and(n == node, u == unit)

                    @pl.when(mine)
                    def _():
                        pltpu.make_async_copy(
                            own.at[p, u, n], home.at[p, expert_here], recv_h.at[p, expert_here]
                        ).start()

                    @pl.when(jnp.logical_not(mine))
                    def _():
                        give_home(p, u, n).start()

            return 0

        lax.fori_loop(0, units, near, 0)

    for p in range(pieces):
        for c in range(cols):
            j = p * cols + c
            outs = [
                dot(hidden, wd[:, q * piece + j * COL : q * piece + (j + 1) * COL]).astype(BF) for q in range(SPLIT)
            ]
            if j < CAP:
                outs.append(last)
            closing = closer(tail_parts[j])
            for u in range(units):
                mine = [o[u * UNIT_ROWS : (u + 1) * UNIT_ROWS] for o in outs]
                halves = dot(closing, jnp.concatenate(mine, axis=0)).astype(BF).reshape(2, nodes, SUB, COL)
                own[p, u, :, :, c * COL : (c + 1) * COL] = halves[0]
                sib[p, u, :, :, c * COL : (c + 1) * COL] = halves[1]
            if c == 0 and p >= 1:
                add_core(p - 1)
        give_half(p).start()
        if p >= 2:
            add_chip(p - 2)
    add_core(pieces - 1)
    for p in range(max(pieces - 2, 0), pieces):
        add_chip(p)

    line = iota((rows, packed), 1)
    slot_t = jnp.transpose(slot_m)
    coef_t = jnp.transpose(coef_m)
    heads = [jnp.where(member(line, slot_t, q), coef_t, 0.0).astype(BF) for q in range(SPLIT)]
    tails = [jnp.where(member_tail(line, slot_t, r), coef_t, 0.0).astype(BF) for r in range(CAP)]
    tail = jnp.zeros((rows, COL), F32)
    for p in range(pieces):
        def returned(e, _):
            landed(home.at[p, e], recv_h.at[p, e])
            return 0

        lax.fori_loop(0, hosted, returned, 0)
        for c in range(cols):
            j = p * cols + c
            got = home[p, :, :, c * COL : (c + 1) * COL].reshape(packed, COL)
            for q in range(SPLIT):
                tok[:, q * piece + j * COL : q * piece + (j + 1) * COL] = dot(heads[q], got).astype(BF)
            if j < CAP:
                tail = tail + dot(tails[j], got)
    tok[:, tail0:] = tail.astype(BF)
    store = pltpu.make_async_copy(tok, out_hbm, in_sem.at[0])
    store.start()

    for p in range(pieces):
        def sent(i, _):
            e, n, to_unit, mine = target(i)

            @pl.when(jnp.logical_not(mine))
            def _():
                dispatch(p, e, n, to_unit).wait_send()

            return 0

        lax.fori_loop(0, hosted, sent, 0)

        def drained(u, _):
            near = is_near(u)
            to_sibling(p, u).wait_send()

            @pl.when(near)
            def _():
                to_partner(p, u).wait_send()
                for n in range(nodes):
                    @pl.when(jnp.logical_or(n != node, u != unit))
                    def _():
                        give_home(p, u, n).wait_send()

            @pl.when(jnp.logical_not(near))
            def _():
                give_sum(p, u).wait_send()

            return 0

        lax.fori_loop(0, units, drained, 0)
        give_half(p).wait_send()
    store.wait()


def on_device(tokens, route_ids, route_gates, limits, w_gate, w_up, w_down):
    nodes = lax.axis_size("node")
    locs = lax.axis_size("local")
    units = locs // 2
    hosted = nodes * (locs // GROUP)
    rows, width = tokens.shape
    slab = w_down.shape[1]
    piece = (width // COL // SPLIT) * COL
    part = piece // PIECES
    assert width - SPLIT * piece == COL and SPLIT * CAP == SUB - 1 and part * PIECES == piece and part % COL == 0
    assert CAP * COL <= piece and hosted <= 128 and 2 * nodes * CAP <= UNIT_ROWS
    xrows = -(-units * UNIT_ROWS // 128) * 128
    block = (SUB, part)
    dma = pltpu.SemaphoreType.DMA
    vmem = pl.BlockSpec(memory_space=pltpu.VMEM)
    hbm = pl.BlockSpec(memory_space=pl.ANY)
    return pl.pallas_call(
        functools.partial(kernel, (nodes, locs)),
        out_shape=jax.ShapeDtypeStruct((rows, width), BF),
        in_specs=[hbm, vmem, vmem, pl.BlockSpec(memory_space=pltpu.SMEM), hbm, hbm, hbm],
        out_specs=hbm,
        scratch_shapes=[
            pltpu.VMEM((rows, width), BF),
            pltpu.VMEM((2 * slab, width), BF),
            pltpu.VMEM((slab, width), BF),
            pltpu.VMEM((PIECES, hosted) + block, BF),
            pltpu.VMEM((PIECES, units, 2, nodes) + block, BF),
            pltpu.VMEM((xrows, SPLIT * part), BF),
            pltpu.VMEM((xrows, COL), BF),
            pltpu.VMEM((2 * slab, xrows), F32),
            pltpu.VMEM((PIECES, units, nodes) + block, BF),
            pltpu.VMEM((PIECES, units, nodes) + block, BF),
            pltpu.VMEM((PIECES, units, nodes) + block, BF),
            pltpu.VMEM((PIECES, units, nodes) + block, BF),
            pltpu.VMEM((PIECES, hosted) + block, BF),
            dma((4,)),
            dma((PIECES, units, nodes)),
            dma((PIECES, units, 2)),
            dma((PIECES, hosted)),
            dma((PIECES, units)),
            dma((PIECES, units)),
            dma((PIECES,)),
            dma((PIECES,)),
            dma((PIECES, units)),
            dma((PIECES, units)),
            dma((PIECES, units, nodes)),
            dma((PIECES, hosted)),
        ],
        compiler_params=pltpu.CompilerParams(
            collective_id=0, has_side_effects=True, vmem_limit_bytes=62 * 1024 * 1024
        ),
        cost_estimate=pl.CostEstimate(
            flops=6 * locs * nodes * CAP * width * slab, bytes_accessed=6 * width * slab, transcendentals=0
        ),
    )(
        tokens,
        route_ids.T,
        route_gates.T,
        limits,
        jnp.swapaxes(w_gate, 1, 2)[0],
        jnp.swapaxes(w_up, 1, 2)[0],
        w_down[0],
    )


def solution(mesh):
    return jax.shard_map(
        on_device,
        mesh=mesh,
        in_specs=(
            P(("node", "local"), None),
            P(("node", "local"), None),
            P(("node", "local"), None),
            P(),
            P(("node", "local"), None, None),
            P(("node", "local"), None, None),
            P(("node", "local"), None, None),
        ),
        out_specs=P(("node", "local"), None),
        check_vma=False,
    )
```

```python
import functools

import jax
import jax.numpy as jnp
from jax import lax
from jax.experimental import pallas as pl
from jax.experimental.pallas import tpu as pltpu
from jax.sharding import PartitionSpec as P

GROUP = 4
CAP = 5
PIECES = 3
UNIT_ROWS = 48
SUB = 16
SPLIT = 3
COL = 256
BF = jnp.bfloat16
F32 = jnp.float32
MESH = pl.DeviceIdType.MESH


def dot(a, b):
    return jnp.dot(a, b, preferred_element_type=F32)


def dot_t(a, b):
    return lax.dot_general(a, b, (((1,), (1,)), ((), ())), preferred_element_type=F32)


def iota(shape, dim):
    return lax.broadcasted_iota(jnp.int32, shape, dim)


def div_cap(x):
    return (x * 205) >> 10


def kernel(
    dims,
    tok_hbm, ids_ref, gates_ref, limits_ref, wg_hbm, wu_hbm, wd_hbm,
    out_hbm,
    tok, wgu, wd, pack, x, xu, xt, both, own, sib, sib_in, par_in, home,
    in_sem, recv_x, recv_g, send_d, send_s, send_r, send_p, recv_p, send_q, recv_q, send_h, recv_h,
):
    nodes, locs = dims
    groups = locs // GROUP
    units = locs // 2
    hosted = nodes * groups
    rows = tok.shape[0]
    pieces, part = x.shape[0], x.shape[-1]
    piece = pieces * part
    tail0 = SPLIT * piece
    cols = part // COL
    packed = hosted * SUB
    chunk = 2 * nodes * SUB
    xrows = xu.shape[0]
    slab = wd.shape[0]

    node = lax.axis_index("node")
    loc = lax.axis_index("local")
    core = lax.rem(loc, 2)
    unit = loc // 2
    place = lax.rem(unit, 2)
    group = unit // 2
    sibling = (node, unit * 2 + (1 - core))
    partner = (node, group * GROUP + 2 * (1 - place) + core)

    loads = [
        pltpu.make_async_copy(tok_hbm, tok, in_sem.at[0]),
        pltpu.make_async_copy(wg_hbm, wgu.at[pl.ds(0, slab)], in_sem.at[1]),
        pltpu.make_async_copy(wu_hbm, wgu.at[pl.ds(slab, slab)], in_sem.at[2]),
        pltpu.make_async_copy(wd_hbm, wd, in_sem.at[3]),
    ]
    loads[0].start()

    barrier = pltpu.get_barrier_semaphore()

    def greet(i, _):
        n, u = i // units, lax.rem(i, units)

        @pl.when(jnp.logical_or(n != node, u != unit))
        def _():
            pl.semaphore_signal(barrier, inc=1, device_id=(n, u * 2 + core), device_id_type=MESH)

        return 0

    lax.fori_loop(0, nodes * units, greet, 0)
    pl.semaphore_signal(barrier, inc=1, device_id=sibling, device_id_type=MESH)

    ep = 128
    expert = iota((ep, rows), 0)
    named = jnp.zeros((ep, rows), F32)
    gate = jnp.zeros((ep, rows), F32)
    for k in range(ids_ref.shape[0]):
        hit = ids_ref[k : k + 1, :] == expert
        named = named + jnp.where(hit, 1.0, 0.0)
        gate = gate + jnp.where(hit, gates_ref[k : k + 1, :].astype(F32), 0.0)
    earlier = jnp.where(iota((rows, rows), 0) < iota((rows, rows), 1), 1.0, 0.0).astype(BF)
    before = dot(named.astype(BF), earlier)
    lim = jnp.zeros((ep, rows), F32)
    for e in range(hosted):
        lim = jnp.where(expert == e, limits_ref[e].astype(F32), lim)
    kept = jnp.logical_and(named > 0.5, before < lim)
    slot = jnp.where(kept, before, -1.0)
    coef = jnp.where(kept, gate, 0.0)
    spread = jnp.where(iota((packed, ep), 0) // SUB == iota((packed, ep), 1), 1.0, 0.0).astype(BF)
    slot_m = dot(spread, slot.astype(BF))
    coef_m = dot(spread, coef.astype(BF))

    def member(line, slots, q):
        row = lax.rem(line, SUB)
        rank = (row * 11) >> 5
        ok = jnp.logical_and(row < SUB - 1, row - SPLIT * rank == q)
        return jnp.logical_and(ok, slots == rank.astype(F32))

    def member_tail(line, slots, r):
        return jnp.logical_and(lax.rem(line, SUB) == SUB - 1, slots == float(r))

    line = iota((packed, rows), 0)
    heads = [jnp.where(member(line, slot_m, q), 1.0, 0.0).astype(BF) for q in range(SPLIT)]
    tails = [jnp.where(member_tail(line, slot_m, r), 1.0, 0.0).astype(BF) for r in range(CAP)]

    loads[0].wait()
    for load in loads[1:]:
        load.start()

    def near_place(src_group, src_place, g):
        return jnp.where(src_group < g, 0, jnp.where(src_group > g, 1, src_place))

    def target(i):
        g = lax.rem(group + lax.rem(i, groups), groups)
        n = lax.rem(node + i // groups, nodes)
        to_unit = 2 * g + near_place(group, place, g)
        e = n * groups + g
        return e, n, to_unit, jnp.logical_and(n == node, to_unit == unit)

    def dispatch(p, e, n, to_unit):
        return pltpu.make_async_remote_copy(
            src_ref=pack.at[p, e], dst_ref=x.at[p, unit, core, node], send_sem=send_d.at[p, e],
            recv_sem=recv_x.at[p, unit, node], device_id=(n, 2 * to_unit + core), device_id_type=MESH,
        )

    def send_piece(p):
        def send_out(i, _):
            e, n, to_unit, mine = target(i)

            @pl.when(mine)
            def _():
                pltpu.make_async_copy(pack.at[p, e], x.at[p, unit, core, node], recv_x.at[p, unit, node]).start()

            @pl.when(jnp.logical_not(mine))
            def _():
                dispatch(p, e, n, to_unit).start()

            return 0

        lax.fori_loop(0, hosted, send_out, 0)

    for p in range(pieces):
        for c in range(cols):
            j = p * cols + c
            acc = dot(heads[0], tok[:, j * COL : (j + 1) * COL])
            for q in range(1, SPLIT):
                acc = acc + dot(heads[q], tok[:, q * piece + j * COL : q * piece + (j + 1) * COL])
            if j < CAP:
                acc = acc + dot(tails[j], tok[:, tail0:])
            pack[p, :, :, c * COL : (c + 1) * COL] = acc.astype(BF).reshape(hosted, SUB, COL)
        if p == 0:
            pl.semaphore_wait(barrier, nodes * units)
            send_piece(0)

    def opener(parts):
        i, m = iota((UNIT_ROWS, chunk), 0), iota((UNIT_ROWS, chunk), 1)
        first, rank = SUB * div_cap(i), i - CAP * div_cap(i)
        out = [m == first + SPLIT * rank + q for q in range(SPLIT)]
        out += [jnp.logical_and(m == first + SUB - 1, rank == r) for r in parts]
        return jnp.concatenate([jnp.where(o, 1.0, 0.0) for o in out], axis=0).astype(BF)

    def closer(parts):
        m, i = iota((chunk, UNIT_ROWS), 0), iota((chunk, UNIT_ROWS), 1)
        blk, sub_row, rank = m // SUB, lax.rem(m, SUB), i - CAP * div_cap(i)
        src = lax.rem(core + blk // nodes, 2) * nodes + lax.rem(blk, nodes)
        same = src == div_cap(i)
        out = [jnp.logical_and(same, sub_row == SPLIT * rank + q) for q in range(SPLIT)]
        out += [jnp.logical_and(same, jnp.logical_and(sub_row == SUB - 1, rank == r)) for r in parts]
        return jnp.concatenate([jnp.where(o, 1.0, 0.0) for o in out], axis=1).astype(BF)

    tail_parts = [[j] if j < CAP else [] for j in range(pieces * cols)]

    def is_near(u):
        return near_place(u // 2, lax.rem(u, 2), group) == place

    def to_sibling(p, u):
        return pltpu.make_async_remote_copy(
            src_ref=x.at[p, u, core], dst_ref=x.at[p, u, core], send_sem=send_s.at[p, u],
            recv_sem=recv_g.at[p, u, core], device_id=sibling, device_id_type=MESH,
        )

    def to_partner(p, u):
        return pltpu.make_async_remote_copy(
            src_ref=x.at[p, u, core], dst_ref=x.at[p, u, core], send_sem=send_r.at[p, u],
            recv_sem=recv_g.at[p, u, core], device_id=partner, device_id_type=MESH,
        )

    def give_half(p):
        return pltpu.make_async_remote_copy(
            src_ref=sib.at[p], dst_ref=sib_in.at[p], send_sem=send_p.at[p],
            recv_sem=recv_p.at[p], device_id=sibling, device_id_type=MESH,
        )

    def give_sum(p, u):
        return pltpu.make_async_remote_copy(
            src_ref=own.at[p, u], dst_ref=par_in.at[p, u], send_sem=send_q.at[p, u],
            recv_sem=recv_q.at[p, u], device_id=partner, device_id_type=MESH,
        )

    expert_here = node * groups + group

    def give_home(p, u, n):
        return pltpu.make_async_remote_copy(
            src_ref=own.at[p, u, n], dst_ref=home.at[p, expert_here], send_sem=send_h.at[p, u, n],
            recv_sem=recv_h.at[p, expert_here], device_id=(n, 2 * u + core), device_id_type=MESH,
        )

    def landed(ref, sem):
        pltpu.make_async_copy(ref, ref, sem).wait()

    def relay_near(p):
        def first(k, _):
            u = lax.rem(2 * group + k, units)

            @pl.when(is_near(u))
            def _():
                for n in range(nodes):
                    landed(x.at[p, u, core, n], recv_x.at[p, u, n])
                to_partner(p, u).start()
                to_sibling(p, u).start()

            return 0

        lax.fori_loop(0, units, first, 0)
        if p + 1 < pieces:
            send_piece(p + 1)

    def relay_far(p):
        def second(k, _):
            u = lax.rem(2 * group + k, units)

            @pl.when(jnp.logical_not(is_near(u)))
            def _():
                landed(x.at[p, u, core], recv_g.at[p, u, core])
                to_sibling(p, u).start()

            return 0

        def third(k, _):
            u = lax.rem(2 * group + k, units)
            landed(x.at[p, u, 1 - core], recv_g.at[p, u, 1 - core])
            return 0

        lax.fori_loop(0, units, second, 0)
        lax.fori_loop(0, units, third, 0)

    if xrows > units * UNIT_ROWS:
        spare = (xrows - units * UNIT_ROWS, xu.shape[1])
        xu[units * UNIT_ROWS :, :] = jnp.zeros(spare, BF)
        xt[units * UNIT_ROWS :, :] = jnp.zeros((spare[0], COL), BF)
    last_tail = (CAP - 1) // cols
    relay_near(0)
    for p in range(pieces):
        relay_far(p)
        for c in range(cols):
            j = p * cols + c
            opening = opener(tail_parts[j])

            def unpack(u, _):
                base = pl.multiple_of(u * UNIT_ROWS, SUB)
                xc = x[p, u, :, :, :, c * COL : (c + 1) * COL].reshape(chunk, COL)
                opened = dot(opening, xc).astype(BF)
                for q in range(SPLIT):
                    xu[pl.ds(base, UNIT_ROWS), q * part + c * COL : q * part + (c + 1) * COL] = opened[
                        q * UNIT_ROWS : (q + 1) * UNIT_ROWS
                    ]
                if j < CAP:
                    more = opened[SPLIT * UNIT_ROWS :]
                    if j > 0:
                        more = xt[pl.ds(base, UNIT_ROWS), :] + more
                    xt[pl.ds(base, UNIT_ROWS), :] = more
                return 0

            lax.fori_loop(0, units, unpack, 0, unroll=True if units <= 4 else 1)
        if p == 0:
            for load in loads[1:]:
                load.wait()
        acc = dot_t(wgu[:, p * part : (p + 1) * part], xu[:, :part])
        both[...] = acc if p == 0 else both[...] + acc
        if p + 1 < pieces:
            relay_near(p + 1)
        acc = dot_t(wgu[:, piece + p * part : piece + (p + 1) * part], xu[:, part : 2 * part])
        for q in range(2, SPLIT):
            at = q * piece + p * part
            acc = acc + dot_t(wgu[:, at : at + part], xu[:, q * part : (q + 1) * part])
        if p == last_tail:
            acc = acc + dot_t(wgu[:, tail0:], xt[...])
        both[...] = both[...] + acc

    act, up = both[:slab], both[slab:]
    hidden_t = (act / (1.0 + jnp.exp(-act)) * up).astype(BF)
    filled = (units * UNIT_ROWS, xrows)
    eye = jnp.where(iota(filled, 0) == iota(filled, 1), 1.0, 0.0).astype(BF)
    hidden = dot_t(eye, hidden_t).astype(BF)
    last = dot(hidden, wd[:, tail0:]).astype(BF)

    def add_core(p):
        landed(sib_in.at[p], recv_p.at[p])

        def far(u, _):
            @pl.when(jnp.logical_not(is_near(u)))
            def _():
                for n in range(nodes):
                    own[p, u, n] = (own[p, u, n].astype(F32) + sib_in[p, u, n].astype(F32)).astype(BF)
                give_sum(p, u).start()

            return 0

        lax.fori_loop(0, units, far, 0)

    def add_chip(p):
        def near(u, _):
            @pl.when(is_near(u))
            def _():
                landed(par_in.at[p, u], recv_q.at[p, u])
                for n in range(nodes):
                    total = own[p, u, n].astype(F32) + sib_in[p, u, n].astype(F32) + par_in[p, u, n].astype(F32)
                    own[p, u, n] = total.astype(BF)
                    mine = jnp.logical_and(n == node, u == unit)

                    @pl.when(mine)
                    def _():
                        pltpu.make_async_copy(
                            own.at[p, u, n], home.at[p, expert_here], recv_h.at[p, expert_here]
                        ).start()

                    @pl.when(jnp.logical_not(mine))
                    def _():
                        give_home(p, u, n).start()

            return 0

        lax.fori_loop(0, units, near, 0)

    for p in range(pieces):
        for c in range(cols):
            j = p * cols + c
            outs = [
                dot(hidden, wd[:, q * piece + j * COL : q * piece + (j + 1) * COL]).astype(BF) for q in range(SPLIT)
            ]
            if j < CAP:
                outs.append(last)
            closing = closer(tail_parts[j])
            for u in range(units):
                mine = [o[u * UNIT_ROWS : (u + 1) * UNIT_ROWS] for o in outs]
                halves = dot(closing, jnp.concatenate(mine, axis=0)).astype(BF).reshape(2, nodes, SUB, COL)
                own[p, u, :, :, c * COL : (c + 1) * COL] = halves[0]
                sib[p, u, :, :, c * COL : (c + 1) * COL] = halves[1]
            if c == 0 and p >= 1:
                add_core(p - 1)
        give_half(p).start()
        if p >= 2:
            add_chip(p - 2)
    add_core(pieces - 1)
    for p in range(max(pieces - 2, 0), pieces):
        add_chip(p)

    line = iota((rows, packed), 1)
    slot_t = jnp.transpose(slot_m)
    coef_t = jnp.transpose(coef_m)
    heads = [jnp.where(member(line, slot_t, q), coef_t, 0.0).astype(BF) for q in range(SPLIT)]
    tails = [jnp.where(member_tail(line, slot_t, r), coef_t, 0.0).astype(BF) for r in range(CAP)]
    tail = jnp.zeros((rows, COL), F32)
    for p in range(pieces):
        def returned(e, _):
            landed(home.at[p, e], recv_h.at[p, e])
            return 0

        lax.fori_loop(0, hosted, returned, 0)
        for c in range(cols):
            j = p * cols + c
            got = home[p, :, :, c * COL : (c + 1) * COL].reshape(packed, COL)
            for q in range(SPLIT):
                tok[:, q * piece + j * COL : q * piece + (j + 1) * COL] = dot(heads[q], got).astype(BF)
            if j < CAP:
                tail = tail + dot(tails[j], got)
    tok[:, tail0:] = tail.astype(BF)
    store = pltpu.make_async_copy(tok, out_hbm, in_sem.at[0])
    store.start()

    for p in range(pieces):
        def sent(i, _):
            e, n, to_unit, mine = target(i)

            @pl.when(jnp.logical_not(mine))
            def _():
                dispatch(p, e, n, to_unit).wait_send()

            return 0

        lax.fori_loop(0, hosted, sent, 0)

        def drained(u, _):
            near = is_near(u)
            to_sibling(p, u).wait_send()

            @pl.when(near)
            def _():
                to_partner(p, u).wait_send()
                for n in range(nodes):
                    @pl.when(jnp.logical_or(n != node, u != unit))
                    def _():
                        give_home(p, u, n).wait_send()

            @pl.when(jnp.logical_not(near))
            def _():
                give_sum(p, u).wait_send()

            return 0

        lax.fori_loop(0, units, drained, 0)
        give_half(p).wait_send()
    store.wait()


def on_device(tokens, route_ids, route_gates, limits, w_gate, w_up, w_down):
    nodes = lax.axis_size("node")
    locs = lax.axis_size("local")
    units = locs // 2
    hosted = nodes * (locs // GROUP)
    rows, width = tokens.shape
    slab = w_down.shape[1]
    piece = (width // COL // SPLIT) * COL
    part = piece // PIECES
    assert width - SPLIT * piece == COL and SPLIT * CAP == SUB - 1 and part * PIECES == piece and part % COL == 0
    assert CAP * COL <= piece and hosted <= 128 and 2 * nodes * CAP <= UNIT_ROWS
    xrows = -(-units * UNIT_ROWS // 128) * 128
    block = (SUB, part)
    dma = pltpu.SemaphoreType.DMA
    vmem = pl.BlockSpec(memory_space=pltpu.VMEM)
    hbm = pl.BlockSpec(memory_space=pl.ANY)
    return pl.pallas_call(
        functools.partial(kernel, (nodes, locs)),
        out_shape=jax.ShapeDtypeStruct((rows, width), BF),
        in_specs=[hbm, vmem, vmem, pl.BlockSpec(memory_space=pltpu.SMEM), hbm, hbm, hbm],
        out_specs=hbm,
        scratch_shapes=[
            pltpu.VMEM((rows, width), BF),
            pltpu.VMEM((2 * slab, width), BF),
            pltpu.VMEM((slab, width), BF),
            pltpu.VMEM((PIECES, hosted) + block, BF),
            pltpu.VMEM((PIECES, units, 2, nodes) + block, BF),
            pltpu.VMEM((xrows, SPLIT * part), BF),
            pltpu.VMEM((xrows, COL), BF),
            pltpu.VMEM((2 * slab, xrows), F32),
            pltpu.VMEM((PIECES, units, nodes) + block, BF),
            pltpu.VMEM((PIECES, units, nodes) + block, BF),
            pltpu.VMEM((PIECES, units, nodes) + block, BF),
            pltpu.VMEM((PIECES, units, nodes) + block, BF),
            pltpu.VMEM((PIECES, hosted) + block, BF),
            dma((4,)),
            dma((PIECES, units, nodes)),
            dma((PIECES, units, 2)),
            dma((PIECES, hosted)),
            dma((PIECES, units)),
            dma((PIECES, units)),
            dma((PIECES,)),
            dma((PIECES,)),
            dma((PIECES, units)),
            dma((PIECES, units)),
            dma((PIECES, units, nodes)),
            dma((PIECES, hosted)),
        ],
        compiler_params=pltpu.CompilerParams(
            collective_id=0, has_side_effects=True, vmem_limit_bytes=62 * 1024 * 1024
        ),
        cost_estimate=pl.CostEstimate(
            flops=6 * locs * nodes * CAP * width * slab, bytes_accessed=6 * width * slab, transcendentals=0
        ),
    )(
        tokens,
        route_ids.T,
        route_gates.T,
        limits,
        jnp.swapaxes(w_gate, 1, 2)[0],
        jnp.swapaxes(w_up, 1, 2)[0],
        w_down[0],
    )


def solution(mesh):
    return jax.shard_map(
        on_device,
        mesh=mesh,
        in_specs=(
            P(("node", "local"), None),
            P(("node", "local"), None),
            P(("node", "local"), None),
            P(),
            P(("node", "local"), None, None),
            P(("node", "local"), None, None),
            P(("node", "local"), None, None),
        ),
        out_specs=P(("node", "local"), None),
        check_vma=False,
    )
```
